32 devices in a mesh: slot: 4 (over x, core), horiz: 8 (over z, y).
Axes of the slice: x: 2, y: 2, z: 4, core: 2. Of those that a mesh axis runs over, the one named last changes fastest.
Arguments:
- control: bfloat16 [32, 80, 16, 128], P(None, None, 'horiz'), may hold values from -6 to 6
- land_mask: int32 [80, 16, 128], P(None, 'horiz'), may hold values 0 or 1
- tile_id: int32 [4, 32], replicated, may hold values from 0 to 15
- tile_scale: float32 [16, 80], replicated, may hold values from 0.3 to 3
- inverse_x: bfloat16 [128, 128], replicated
- inverse_y: bfloat16 [16, 16], replicated
- inverse_z: bfloat16 [80, 80], replicated
- perturbations: bfloat16 [4, 32, 80, 16, 128], P('slot', None, None, 'horiz'), may hold values from -6 to 6
- obs_cell: int32 [4, 65536], P('slot', 'horiz'), may hold values from 0 to 20479
- obs_value: float32 [4, 65536], P('slot', 'horiz'), may hold values from -6 to 6
- obs_weight: float32 [4, 65536], P('slot', 'horiz'), may hold values from 1 to 8
Outputs:
- gradient: bfloat16 [32, 80, 16, 128], P(None, None, 'horiz')
The draws below stay inside these ranges and needn't reach their ends.
Inputs may be any that keep to these rules, and one draw needn't show every extreme that they name: obs_cell[s, j] indexes the cells of tile j // 8192 (rows j // 8192 * 2 onward), level-major, then row, then column.
All inputs are finite; a program needn't handle non-finite values. No bound on the sum of `land_mask` on one device may be relied on, other than what follows from the above.
Results may differ from the reference program's by a relative error of at most 0.006.
Values may be sent and summed in bfloat16 or wider, within the bound.
A program may use at most 192 MiB of HBM per device.

```python
import math
import jax
import jax.numpy as jnp
from jax import lax

M = 32
Z = 80
REGIONS = 16
ROWS_DEV = 2
OBS_DEV = 8192
NX = 128
NY = 16
SLOTS = 4
NOBS = 65536


def line_inverse(key, count, length, spread, power):
    positions = jnp.arange(count, dtype=jnp.float32)
    distance = jnp.abs(positions[:, None] - positions[None, :])
    kernel = jnp.exp(-distance / length)
    jitter = jax.random.uniform(key, (count, count), jnp.float32, -1.0, 1.0)
    factor = 1.0 + spread * jnp.sign(jitter) * jnp.abs(jitter) ** power
    return (kernel * factor / jnp.sqrt(jnp.float32(length))).astype(jnp.bfloat16)


def draw_inverse_x(key, part):
    key = jax.random.fold_in(key, 11)
    return line_inverse(key, NX, max(NX // 4, 1) * 1.0, 0.4, 1.0)


def draw_inverse_y(key, part):
    key = jax.random.fold_in(key, 23)
    return line_inverse(key, NY, max(NY // 4, 1) * 1.0, 0.4, 1.0)


def draw_inverse_z(key, part):
    key = jax.random.fold_in(key, 37)
    return line_inverse(key, Z, max(Z // 8, 1) * 1.0, 0.4, 1.0)


def plant(result, stream_key, least, top_value):
    place = [jax.random.randint(jax.random.fold_in(stream_key, axis), (), 0, length) for axis, length in enumerate(result.shape)]
    main_axis = result.shape.index(max(result.shape))
    neighbour = place[:main_axis] + [(place[main_axis] + 1) % result.shape[main_axis]] + place[main_axis + 1:]
    return result.at[tuple(place)].set(least).at[tuple(neighbour)].set(top_value)


def block_levels(stream_key, extent, shards, low, largest):
    def one(axis_at, blocks):
        draws = jax.random.uniform(jax.random.fold_in(jax.random.fold_in(stream_key, 6), axis_at), (blocks,), jnp.float32, low / len(shards), largest / len(shards))
        return jnp.repeat(jnp.exp(draws), extent[axis_at] // blocks).reshape((-1,) + (1,) * (len(extent) - axis_at - 1))

    gain = one(*shards[0])
    for cut in shards[1:]:
        gain = gain * one(*cut)
    return gain


def centred(stream_key, extent, deviation, limit, shards=(), kind=jnp.bfloat16):
    array = jax.random.normal(stream_key, extent, jnp.float32) * deviation
    if len(shards) > 0:
        array = block_levels(stream_key, extent, shards, -0.22, 0.18) * array
    return jnp.clip(array, min=-limit, max=limit).astype(kind)


def setup_inputs(seed: int = 0) -> dict:
    streams_of = jax.random.split(jax.random.key(seed), 12)
    return {
        "control": centred(streams_of[0], (M, Z, NY, NX), 1.0, 6.0, ((2, 8),)),
        "land_mask": plant((jax.random.randint(streams_of[1], (Z, NY, NX), 0, 5) < 4).astype(jnp.int32), jax.random.fold_in(streams_of[1], 1), 0, 1),
        "tile_id": plant(jax.random.randint(streams_of[2], (NY // 4, NX // 4), 0, REGIONS), jax.random.fold_in(streams_of[2], 1), 0, REGIONS - 1).astype(jnp.int32),
        "tile_scale": jnp.clip(jnp.exp(jax.random.uniform(streams_of[3], (REGIONS, Z), jnp.float32, math.log(0.3), math.log(3.0))), 0.3, 3.0),
        "inverse_x": draw_inverse_x(jax.random.fold_in(streams_of[11], 71), 0),
        "inverse_y": draw_inverse_y(jax.random.fold_in(streams_of[11], 71), 0),
        "inverse_z": draw_inverse_z(jax.random.fold_in(streams_of[11], 71), 0),
        "perturbations": centred(streams_of[7], (SLOTS, M, Z, NY, NX), 1.0, 6.0, ((0, 4), (3, 8))),
        "obs_cell": plant(jax.random.randint(streams_of[8], (SLOTS, NOBS), 0, Z * ROWS_DEV * NX), jax.random.fold_in(streams_of[8], 1), 0, (Z * ROWS_DEV * NX) - 1).astype(jnp.int32),
        "obs_value": centred(streams_of[9], (SLOTS, NOBS), 1.0, 6.0, ((0, 4), (1, 8)), jnp.float32),
        "obs_weight": jnp.clip(jnp.exp(math.log(8.0) - 2.0794415 * jax.random.uniform(streams_of[10], (SLOTS, NOBS), jnp.float32) ** block_levels(streams_of[10], (SLOTS, NOBS), ((0, 4), (1, 8)), -0.2, 0.2)), 1.0, 8.0),
    }


def cell_sigma(tile_id, tile_scale):
    row_tile = jnp.arange(NY, dtype=jnp.int32) // 4
    col_tile = jnp.arange(NX, dtype=jnp.int32) // 4
    region = tile_id[row_tile][:, col_tile]
    return jnp.transpose(tile_scale[region], (2, 0, 1)).astype(jnp.float32)

def forward_filter(control, sea_mask, weight_mask, inverse_x, inverse_y, inverse_z):
    masked = (weight_mask * control.astype(jnp.float32)).astype(jnp.bfloat16)
    along_x = (sea_mask * jnp.einsum('mzyx,xk->mzyk', masked.astype(jnp.float32), inverse_x.astype(jnp.float32))).astype(jnp.bfloat16)
    across = jnp.einsum('mzyx,yk->mzkx', along_x.astype(jnp.float32), inverse_y.astype(jnp.float32)).astype(jnp.bfloat16)
    deeper = jnp.einsum('mzyx,zk->mkyx', across.astype(jnp.float32), inverse_z.astype(jnp.float32)).astype(jnp.bfloat16)
    return deeper * sea_mask.astype(jnp.bfloat16)

def adjoint_filter(slot_sum, sea_mask, weight_mask, inverse_x, inverse_y, inverse_z):
    back_first = (sea_mask * slot_sum).astype(jnp.bfloat16)
    back_deep = jnp.einsum('mkyx,zk->mzyx', back_first.astype(jnp.float32), inverse_z.astype(jnp.float32)).astype(jnp.bfloat16)
    back_across = (sea_mask * jnp.einsum('mzkx,yk->mzyx', back_deep.astype(jnp.float32), inverse_y.astype(jnp.float32))).astype(jnp.bfloat16)
    along_x = jnp.einsum('mzyk,xk->mzyx', back_across.astype(jnp.float32), inverse_x.astype(jnp.float32))
    return weight_mask * along_x

def reference(control, land_mask, tile_id, tile_scale, inverse_x, inverse_y, inverse_z, perturbations, obs_cell, obs_value, obs_weight):
    sea_mask = land_mask.astype(jnp.float32)
    weight_mask = sea_mask * cell_sigma(tile_id, tile_scale)
    spread_w = forward_filter(control, sea_mask, weight_mask, inverse_x, inverse_y, inverse_z)
    norm_scale = 1.0 / math.sqrt(M)
    tile_num = jnp.arange(NOBS, dtype=jnp.int32) // OBS_DEV
    slot_sum = jnp.zeros((M, Z, NY, NX), jnp.float32)
    for slot_num in range(SLOTS):
        perturbed = perturbations[slot_num].astype(jnp.float32)
        increment = lax.optimization_barrier(jnp.sum(perturbed * spread_w.astype(jnp.float32), axis=0)) * norm_scale
        local_cell = obs_cell[slot_num].astype(jnp.int32)
        level = local_cell // (ROWS_DEV * NX)
        row_num = local_cell // NX % ROWS_DEV
        col_num = local_cell % NX
        flat_cell = ((level * NY + tile_num * ROWS_DEV + row_num) * NX + col_num).astype(jnp.int32)
        observed = increment.reshape(-1)[flat_cell]
        misfit = obs_weight[slot_num] * (observed - obs_value[slot_num])
        adjoint_obs = jnp.zeros((Z * NY * NX,), jnp.float32).at[flat_cell].add(misfit).reshape(Z, NY, NX)
        slot_sum = slot_sum + perturbed * (adjoint_obs * norm_scale)[None]
    filtered = adjoint_filter(slot_sum, sea_mask, weight_mask, inverse_x, inverse_y, inverse_z)
    return (control.astype(jnp.float32) + filtered).astype(jnp.bfloat16)
```

```python
import functools
import math

import jax
import jax.numpy as jnp
from jax import lax
from jax.experimental import pallas as pl
from jax.experimental.pallas import tpu as pltpu
from jax.sharding import PartitionSpec as P

LANES = 128
GROUP = 16
F32 = jnp.float32
BF16 = jnp.bfloat16
MESH = pl.DeviceIdType.MESH


def dot(a, b, ca=1, cb=0, precision=None):
    return lax.dot_general(
        a, b, (((ca,), (cb,)), ((), ())), preferred_element_type=F32, precision=precision
    )


def iota(shape, dim):
    return lax.broadcasted_iota(jnp.int32, shape, dim)


def spread_matrix(shape, index):
    return jnp.where(index == iota(shape, 1), 1.0, 0.0).astype(BF16)


def kernel(
    slots,
    tiles,
    rows,
    control,
    land,
    tile_id,
    tile_scale,
    inv_x,
    inv_y,
    inv_z,
    pert,
    cells,
    values,
    weights,
    out,
    sea,
    weight,
    ky,
    ky_t,
    kz,
    kz_t,
    obs_acc,
    inc,
    adj,
    send_a,
    recv_a,
    across,
    send_b,
    spread,
    stage_c,
    recv_c,
    stage_x,
    recv_x,
    stage_d,
    recv_d,
    deep,
    stage_e,
    recv_e,
    tile_ss,
    tile_rs,
    gather_ss,
    gather_rs,
    red_ss,
    red_rs,
):
    members, depth, cols = control.shape
    own = members // slots
    blocks = cols // LANES
    levels = depth // rows
    s = lax.axis_index("slot")
    h = lax.axis_index("horiz")
    sib = s + 1 - 2 * lax.rem(s, 2)
    far = s + 2 - 4 * (s // 2)
    diag = sib + 2 - 4 * (sib // 2)

    barrier = pltpu.get_barrier_semaphore()
    for d in range(1, tiles):
        pl.semaphore_signal(
            barrier, inc=1, device_id={"horiz": lax.rem(h + d, tiles)}, device_id_type=MESH
        )
    for peer in (sib, far):
        pl.semaphore_signal(barrier, inc=1, device_id={"slot": peer}, device_id_type=MESH)

    region = tile_id[pl.ds(h * rows // 4, 1), :].astype(F32).astype(BF16)
    blocks_x = tile_id.shape[1]
    widen = jnp.where(iota((blocks_x, cols), 1) // 4 == iota((blocks_x, cols), 0), 1.0, 0.0)
    region_x = dot(region, widen.astype(BF16))
    regions = tile_scale.shape[0]
    onehot = jnp.where(
        iota((regions, cols), 0).astype(F32) == region_x, 1.0, 0.0
    )
    to_level = spread_matrix((depth, levels), iota((depth, levels), 0) // rows)
    scale_rows = dot(
        to_level.astype(F32), tile_scale[...], 1, 1, precision=lax.Precision.HIGHEST
    )
    sea[...] = land[...].astype(F32)
    weight[...] = sea[...] * dot(scale_rows, onehot, precision=lax.Precision.HIGHEST)

    def at_block(ref, c):
        if blocks == 1:
            return ref[...]
        return ref[:, pl.ds(pl.multiple_of(c * LANES, LANES), LANES)]

    def member_block(ref, m, c):
        if blocks == 1:
            return ref[m]
        return ref[m, :, pl.ds(pl.multiple_of(c * LANES, LANES), LANES)]

    def to_tile(phase, d, src, dst):
        return pltpu.make_async_remote_copy(
            src_ref=src,
            dst_ref=dst,
            send_sem=tile_ss.at[phase, d],
            recv_sem=tile_rs.at[phase, d],
            device_id={"horiz": lax.rem(h + d, tiles)},
            device_id_type=MESH,
        )

    def to_slot(ss, rs, phase, d, src, dst, peer):
        return pltpu.make_async_remote_copy(
            src_ref=src,
            dst_ref=dst,
            send_sem=ss.at[phase, d],
            recv_sem=rs.at[phase, d],
            device_id={"slot": peer},
            device_id_type=MESH,
        )

    order = list(range(1, tiles)) + [0]

    first = []
    for d in order:
        u = lax.rem(h + d, tiles)
        k, c = u // blocks, lax.rem(u, blocks)
        masked = (weight[...] * control[s * own + k].astype(F32)).astype(BF16)
        along = (at_block(sea, c) * dot(masked, at_block(inv_x, c))).astype(BF16)
        if d == 0:
            recv_a[h] = along
        else:
            send_a[u] = along
            if d == 1:
                pl.semaphore_wait(barrier, tiles - 1 + 2)
            copy = to_tile(0, d, send_a.at[u], recv_a.at[h])
            copy.start()
            first.append(copy)

    wide = tiles * GROUP
    side = tiles * rows
    pos = iota((wide, side), 0)
    pick_y = spread_matrix((wide, side), pos // GROUP * rows + lax.rem(pos, rows))
    row_i, col_i = iota((wide, wide), 0), iota((wide, wide), 1)
    same = lax.rem(row_i, GROUP) // rows == lax.rem(col_i, GROUP) // rows
    half = dot(pick_y, inv_y[...]).astype(BF16)
    ky[...] = jnp.where(same, dot(half, pick_y, 1, 1), 0.0).astype(BF16)
    half = dot(pick_y, inv_y[...], 1, 1).astype(BF16)
    ky_t[...] = jnp.where(same, dot(half, pick_y, 1, 1), 0.0).astype(BF16)
    same = lax.rem(iota((depth, depth), 0), rows) == lax.rem(iota((depth, depth), 1), rows)
    half = dot(to_level, inv_z[...]).astype(BF16)
    kz[...] = jnp.where(same, dot(half, to_level, 1, 1), 0.0).astype(BF16)
    half = dot(to_level, inv_z[...], 1, 1).astype(BF16)
    kz_t[...] = jnp.where(same, dot(half, to_level, 1, 1), 0.0).astype(BF16)

    def filter_y(matrix, src, dst):
        for g in range(depth // GROUP):
            part = src[:, g * GROUP : (g + 1) * GROUP, :].reshape(wide, LANES)
            dst[:, g * GROUP : (g + 1) * GROUP, :] = (
                dot(matrix[...], part).astype(BF16).reshape(tiles, GROUP, LANES)
            )

    for copy in first:
        copy.wait_recv()
    filter_y(ky_t, recv_a, across)
    second = []
    for d in order:
        u = lax.rem(h + d, tiles)
        deeper = dot(kz_t[...], across[u]).astype(BF16)
        if d == 0:
            spread[s * tiles + h] = deeper
        else:
            send_b[u] = deeper
            copy = to_tile(1, d, send_b.at[u], spread.at[s * tiles + h])
            copy.start()
            second.append(copy)

    count = cells.shape[1]
    step = min(1024, count)
    shift = cols.bit_length() - 1
    obs_acc[...] = jnp.zeros_like(obs_acc)

    def observe(i, carry):
        where = pl.ds(pl.multiple_of(i * step, step), step)
        cell, w = cells[:, where], weights[:, where]
        wv = w * values[:, where]
        w_hi = w.astype(BF16).astype(F32)
        v_hi = wv.astype(BF16).astype(F32)
        on_row = jnp.where(iota((depth, step), 0) == (cell >> shift), 1.0, 0.0).astype(BF16)
        on_col = iota((cols, step), 0) == (cell & (cols - 1))
        parts = [
            jnp.where(on_col, part, 0.0).astype(BF16) for part in (w_hi, w - w_hi, v_hi, wv - v_hi)
        ]
        for n, part in enumerate(parts):
            obs_acc[n // 2] += dot(on_row, part, 1, 1)
        return carry

    lax.fori_loop(0, count // step, observe, 0)

    inc[...] = jnp.zeros_like(inc)

    def add_member(slot, unit):
        k, c = unit // blocks, lax.rem(unit, blocks)
        term = (
            member_block(pert, slot * own + k, c).astype(F32)
            * spread[slot * tiles + unit].astype(F32)
        )
        if blocks == 1:
            inc[...] += term
        else:
            inc[:, pl.ds(pl.multiple_of(c * LANES, LANES), LANES)] += term

    def source(d):
        return lax.rem(h - d + tiles, tiles)

    def gather_copy(phase, d, unit, peer, buf):
        return to_slot(gather_ss, gather_rs, phase, d, buf.at[unit], buf.at[unit], peer)

    arrive = [0] + list(range(1, tiles))
    core1, far1, fwd1 = [], [], []
    for d in arrive:
        if d > 0:
            second[d - 1].wait_recv()
        unit = s * tiles + source(d)
        far1.append(gather_copy(1, d, unit, far, spread))
        far1[-1].start()
        core1.append(gather_copy(0, d, unit, sib, spread))
        core1[-1].start()
        add_member(s, source(d))
    for d in arrive:
        far1[d].wait_recv()
        fwd1.append(gather_copy(2, d, far * tiles + source(d), sib, spread))
        fwd1[-1].start()
        add_member(far, source(d))
    for d in arrive:
        core1[d].wait_recv()
        add_member(sib, source(d))
    for d in arrive:
        fwd1[d].wait_recv()
        add_member(diag, source(d))

    norm = 1.0 / math.sqrt(members)
    adj[...] = sea[...] * ((inc[...] * norm * obs_acc[0] - obs_acc[1]) * norm)

    def partial(slot, u):
        k, c = u // blocks, lax.rem(u, blocks)
        return member_block(pert, slot * own + k, c).astype(F32) * at_block(adj, c)

    core2, near2, far2 = [], [], []
    for d in order:
        u = lax.rem(h + d, tiles)
        stage_c[u] = partial(diag, u).astype(BF16)
        core2.append(to_slot(red_ss, red_rs, 0, d, stage_c.at[u], recv_c.at[u], sib))
        core2[-1].start()
    for d in order:
        u = lax.rem(h + d, tiles)
        stage_c[tiles + u] = partial(sib, u).astype(BF16)
        near2.append(
            to_slot(red_ss, red_rs, 1, d, stage_c.at[tiles + u], recv_c.at[tiles + u], sib)
        )
        near2[-1].start()
    for n, d in enumerate(order):
        u = lax.rem(h + d, tiles)
        core2[n].wait_recv()
        stage_x[u] = (partial(far, u) + recv_c[u].astype(F32)).astype(BF16)
        far2.append(to_slot(red_ss, red_rs, 2, d, stage_x.at[u], recv_x.at[u], far))
        far2[-1].start()
    third = []
    for n, d in enumerate(order):
        u = lax.rem(h + d, tiles)
        near2[n].wait_recv()
        far2[n].wait_recv()
        total = partial(s, u) + recv_c[tiles + u].astype(F32) + recv_x[u].astype(F32)
        if d == 0:
            recv_d[h] = total.astype(BF16)
        else:
            stage_d[u] = total.astype(BF16)
            copy = to_tile(2, d, stage_d.at[u], recv_d.at[h])
            copy.start()
            third.append(copy)

    for d in arrive:
        if d > 0:
            third[d - 1].wait_recv()
        deep[source(d)] = dot(kz[...], recv_d[source(d)]).astype(BF16)
    filter_y(ky, deep, stage_e)
    fourth = []
    for d in order:
        u = lax.rem(h + d, tiles)
        if d == 0:
            recv_e[h] = stage_e[h]
        else:
            copy = to_tile(3, d, stage_e.at[u], recv_e.at[h])
            copy.start()
            fourth.append(copy)

    if blocks > 1:
        for copy in fourth:
            copy.wait_recv()
    core3, far3, fwd3 = [], [], []
    for n in range(own):
        if blocks == 1:
            if n > 0:
                fourth[n - 1].wait_recv()
            k = source(n)
            field = recv_e[k]
        else:
            k = n
            field = jnp.concatenate([recv_e[n * blocks + c] for c in range(blocks)], axis=1)
        field = (field.astype(F32) * sea[...]).astype(BF16)
        m = s * own + k
        out[m] = (
            control[m].astype(F32) + weight[...] * dot(field, inv_x[...], 1, 1)
        ).astype(BF16)
        far3.append(gather_copy(4, n, m, far, out))
        far3[-1].start()
        core3.append(gather_copy(3, n, m, sib, out))
        core3[-1].start()
    for n in range(own):
        k = source(n) if blocks == 1 else n
        far3[n].wait_recv()
        fwd3.append(gather_copy(5, n, far * own + k, sib, out))
        fwd3[-1].start()
    for n in range(own):
        core3[n].wait_recv()
        fwd3[n].wait_recv()
    for copy in (
        first + second + third + fourth + core1 + far1 + fwd1 + core2 + near2 + far2 + core3
        + far3 + fwd3
    ):
        copy.wait_send()


def per_device(
    slots,
    tiles,
    control,
    land_mask,
    tile_id,
    tile_scale,
    inverse_x,
    inverse_y,
    inverse_z,
    perturbations,
    obs_cell,
    obs_value,
    obs_weight,
):
    members, levels, rows, cols = control.shape
    depth = levels * rows
    blocks = cols // LANES
    assert slots == 4 and cols % LANES == 0 and cols & (cols - 1) == 0
    assert members // slots * blocks == tiles and depth % GROUP == 0 and 4 % rows == 0
    unit = (depth, LANES)
    vmem = pl.BlockSpec(memory_space=pltpu.VMEM)
    gradient = pl.pallas_call(
        functools.partial(kernel, slots, tiles, rows),
        out_shape=jax.ShapeDtypeStruct((members, depth, cols), BF16),
        in_specs=[vmem] * 11,
        out_specs=vmem,
        scratch_shapes=[
            pltpu.VMEM((depth, cols), F32),
            pltpu.VMEM((depth, cols), F32),
            pltpu.VMEM((tiles * GROUP, tiles * GROUP), BF16),
            pltpu.VMEM((tiles * GROUP, tiles * GROUP), BF16),
            pltpu.VMEM((depth, depth), BF16),
            pltpu.VMEM((depth, depth), BF16),
            pltpu.VMEM((2, depth, cols), F32),
            pltpu.VMEM((depth, cols), F32),
            pltpu.VMEM((depth, cols), F32),
            pltpu.VMEM((tiles,) + unit, BF16),
            pltpu.VMEM((tiles,) + unit, BF16),
            pltpu.VMEM((tiles,) + unit, BF16),
            pltpu.VMEM((tiles,) + unit, BF16),
            pltpu.VMEM((slots * tiles,) + unit, BF16),
            pltpu.VMEM((2 * tiles,) + unit, BF16),
            pltpu.VMEM((2 * tiles,) + unit, BF16),
            pltpu.VMEM((tiles,) + unit, BF16),
            pltpu.VMEM((tiles,) + unit, BF16),
            pltpu.VMEM((tiles,) + unit, BF16),
            pltpu.VMEM((tiles,) + unit, BF16),
            pltpu.VMEM((tiles,) + unit, BF16),
            pltpu.VMEM((tiles,) + unit, BF16),
            pltpu.VMEM((tiles,) + unit, BF16),
            pltpu.SemaphoreType.DMA((4, tiles)),
            pltpu.SemaphoreType.DMA((4, tiles)),
            pltpu.SemaphoreType.DMA((6, tiles)),
            pltpu.SemaphoreType.DMA((6, tiles)),
            pltpu.SemaphoreType.DMA((3, tiles)),
            pltpu.SemaphoreType.DMA((3, tiles)),
        ],
        compiler_params=pltpu.CompilerParams(
            collective_id=0, has_side_effects=True, vmem_limit_bytes=56 * 1024 * 1024
        ),
    )(
        control.reshape(members, depth, cols),
        land_mask.reshape(depth, cols),
        tile_id,
        tile_scale,
        inverse_x,
        inverse_y,
        inverse_z,
        perturbations.reshape(members, depth, cols),
        obs_cell,
        obs_value,
        obs_weight,
    )
    return gradient.reshape(members, levels, rows, cols)


def solution(mesh):
    return jax.shard_map(
        functools.partial(per_device, mesh.shape["slot"], mesh.shape["horiz"]),
        mesh=mesh,
        in_specs=(
            P(None, None, "horiz", None),
            P(None, "horiz", None),
            P(),
            P(),
            P(),
            P(),
            P(),
            P("slot", None, None, "horiz", None),
            P("slot", "horiz"),
            P("slot", "horiz"),
            P("slot", "horiz"),
        ),
        out_specs=P(None, None, "horiz", None),
        check_vma=False,
    )
```

```python
import functools
import math

import jax
import jax.numpy as jnp
from jax import lax
from jax.experimental import pallas as pl
from jax.experimental.pallas import tpu as pltpu
from jax.sharding import PartitionSpec as P

LANES = 128
GROUP = 16
F32 = jnp.float32
BF16 = jnp.bfloat16
MESH = pl.DeviceIdType.MESH


def dot(a, b, ca=1, cb=0, precision=None):
    return lax.dot_general(
        a, b, (((ca,), (cb,)), ((), ())), preferred_element_type=F32, precision=precision
    )


def iota(shape, dim):
    return lax.broadcasted_iota(jnp.int32, shape, dim)


def spread_matrix(shape, index):
    return jnp.where(index == iota(shape, 1), 1.0, 0.0).astype(BF16)


def kernel(
    slots,
    tiles,
    rows,
    control_hbm,
    land,
    tile_id,
    tile_scale,
    inv_x,
    inv_y,
    inv_z,
    pert_hbm,
    cells,
    values,
    weights,
    out,
    control,
    pert,
    sea,
    weight,
    ky,
    ky_t,
    kz,
    kz_t,
    obs_acc,
    inc,
    adj,
    send_a,
    recv_a,
    across,
    send_b,
    spread,
    stage_c,
    recv_c,
    stage_x,
    recv_x,
    stage_d,
    recv_d,
    deep,
    stage_e,
    recv_e,
    tile_ss,
    tile_rs,
    gather_ss,
    gather_rs,
    red_ss,
    red_rs,
    load_sem,
):
    members, depth, cols = control_hbm.shape
    own = members // slots
    blocks = cols // LANES
    levels = depth // rows
    s = lax.axis_index("slot")
    h = lax.axis_index("horiz")
    sib = s + 1 - 2 * lax.rem(s, 2)
    far = s + 2 - 4 * (s // 2)
    diag = sib + 2 - 4 * (sib // 2)

    barrier = pltpu.get_barrier_semaphore()
    for d in range(1, tiles):
        pl.semaphore_signal(
            barrier, inc=1, device_id={"horiz": lax.rem(h + d, tiles)}, device_id_type=MESH
        )
    for peer in (sib, far):
        pl.semaphore_signal(barrier, inc=1, device_id={"slot": peer}, device_id_type=MESH)

    load_control = pltpu.make_async_copy(
        control_hbm.at[pl.ds(s * own, own)], control, load_sem.at[0]
    )
    load_pert = pltpu.make_async_copy(pert_hbm, pert, load_sem.at[1])
    load_control.start()
    load_pert.start()

    region = tile_id[pl.ds(h * rows // 4, 1), :].astype(F32).astype(BF16)
    blocks_x = tile_id.shape[1]
    widen = jnp.where(iota((blocks_x, cols), 1) // 4 == iota((blocks_x, cols), 0), 1.0, 0.0)
    region_x = dot(region, widen.astype(BF16))
    regions = tile_scale.shape[0]
    onehot = jnp.where(
        iota((regions, cols), 0).astype(F32) == region_x, 1.0, 0.0
    )
    to_level = spread_matrix((depth, levels), iota((depth, levels), 0) // rows)
    scale_rows = dot(
        to_level.astype(F32), tile_scale[...], 1, 1, precision=lax.Precision.HIGHEST
    )
    sea[...] = land[...].astype(F32)
    weight[...] = sea[...] * dot(scale_rows, onehot, precision=lax.Precision.HIGHEST)

    def at_block(ref, c):
        if blocks == 1:
            return ref[...]
        return ref[:, pl.ds(pl.multiple_of(c * LANES, LANES), LANES)]

    def member_block(ref, m, c):
        if blocks == 1:
            return ref[m]
        return ref[m, :, pl.ds(pl.multiple_of(c * LANES, LANES), LANES)]

    def to_tile(phase, d, src, dst):
        return pltpu.make_async_remote_copy(
            src_ref=src,
            dst_ref=dst,
            send_sem=tile_ss.at[phase, d],
            recv_sem=tile_rs.at[phase, d],
            device_id={"horiz": lax.rem(h + d, tiles)},
            device_id_type=MESH,
        )

    def to_slot(ss, rs, phase, d, src, dst, peer):
        return pltpu.make_async_remote_copy(
            src_ref=src,
            dst_ref=dst,
            send_sem=ss.at[phase, d],
            recv_sem=rs.at[phase, d],
            device_id={"slot": peer},
            device_id_type=MESH,
        )

    order = sorted(range(1, tiles), key=lambda d: abs(2 * d - tiles)) + [0]
    place = {d: n for n, d in enumerate(order)}
    arrive = [0] + order[:-1]

    first = []
    load_control.wait()
    for d in order:
        u = lax.rem(h + d, tiles)
        k, c = u // blocks, lax.rem(u, blocks)
        masked = (weight[...] * control[k].astype(F32)).astype(BF16)
        along = (at_block(sea, c) * dot(masked, at_block(inv_x, c))).astype(BF16)
        if d == 0:
            recv_a[h] = along
        else:
            send_a[u] = along
            if d == order[0]:
                pl.semaphore_wait(barrier, tiles - 1 + 2)
            copy = to_tile(0, d, send_a.at[u], recv_a.at[h])
            copy.start()
            first.append(copy)

    wide = tiles * GROUP
    side = tiles * rows
    pos = iota((wide, side), 0)
    pick_y = spread_matrix((wide, side), pos // GROUP * rows + lax.rem(pos, rows))
    row_i, col_i = iota((wide, wide), 0), iota((wide, wide), 1)
    same = lax.rem(row_i, GROUP) // rows == lax.rem(col_i, GROUP) // rows
    half = dot(pick_y, inv_y[...]).astype(BF16)
    ky[...] = jnp.where(same, dot(half, pick_y, 1, 1), 0.0).astype(BF16)
    half = dot(pick_y, inv_y[...], 1, 1).astype(BF16)
    ky_t[...] = jnp.where(same, dot(half, pick_y, 1, 1), 0.0).astype(BF16)
    same = lax.rem(iota((depth, depth), 0), rows) == lax.rem(iota((depth, depth), 1), rows)
    half = dot(to_level, inv_z[...]).astype(BF16)
    kz[...] = jnp.where(same, dot(half, to_level, 1, 1), 0.0).astype(BF16)
    half = dot(to_level, inv_z[...], 1, 1).astype(BF16)
    kz_t[...] = jnp.where(same, dot(half, to_level, 1, 1), 0.0).astype(BF16)

    def filter_y(matrix, src, dst):
        for g in range(depth // GROUP):
            part = src[:, g * GROUP : (g + 1) * GROUP, :].reshape(wide, LANES)
            dst[:, g * GROUP : (g + 1) * GROUP, :] = (
                dot(matrix[...], part).astype(BF16).reshape(tiles, GROUP, LANES)
            )

    count = cells.shape[1]
    step = min(1024, count)
    shift = cols.bit_length() - 1
    obs_acc[...] = jnp.zeros_like(obs_acc)

    def observe(i, carry):
        where = pl.ds(pl.multiple_of(i * step, step), step)
        cell, w = cells[:, where], weights[:, where]
        wv = w * values[:, where]
        w_hi = w.astype(BF16).astype(F32)
        v_hi = wv.astype(BF16).astype(F32)
        on_row = jnp.where(iota((depth, step), 0) == (cell >> shift), 1.0, 0.0).astype(BF16)
        on_col = iota((cols, step), 0) == (cell & (cols - 1))
        parts = [
            jnp.where(on_col, part, 0.0).astype(BF16) for part in (w_hi, w - w_hi, v_hi, wv - v_hi)
        ]
        for n, part in enumerate(parts):
            obs_acc[n // 2] += dot(on_row, part, 1, 1)
        return carry

    chunks = count // step
    lax.fori_loop(0, chunks // 2, observe, 0)

    for copy in first:
        copy.wait_recv()
    filter_y(ky_t, recv_a, across)
    second = []
    for d in order:
        u = lax.rem(h + d, tiles)
        deeper = dot(kz_t[...], across[u]).astype(BF16)
        if d == 0:
            spread[s * tiles + h] = deeper
        else:
            send_b[u] = deeper
            copy = to_tile(1, d, send_b.at[u], spread.at[s * tiles + h])
            copy.start()
            second.append(copy)


    inc[...] = jnp.zeros_like(inc)

    def add_member(slot, unit):
        k, c = unit // blocks, lax.rem(unit, blocks)
        term = (
            member_block(pert, slot * own + k, c).astype(F32)
            * spread[slot * tiles + unit].astype(F32)
        )
        if blocks == 1:
            inc[...] += term
        else:
            inc[:, pl.ds(pl.multiple_of(c * LANES, LANES), LANES)] += term

    def source(d):
        return lax.rem(h - d + tiles, tiles)

    def gather_copy(phase, d, unit, peer, buf):
        return to_slot(gather_ss, gather_rs, phase, d, buf.at[unit], buf.at[unit], peer)

    core1, far1, fwd1 = [], [], []
    load_pert.wait()
    for n, d in enumerate(arrive):
        if d > 0:
            second[place[d]].wait_recv()
        unit = s * tiles + source(d)
        far1.append(gather_copy(1, n, unit, far, spread))
        far1[-1].start()
        core1.append(gather_copy(0, n, unit, sib, spread))
        core1[-1].start()
        add_member(s, source(d))
    lax.fori_loop(chunks // 2, chunks, observe, 0)
    for n, d in enumerate(arrive):
        far1[n].wait_recv()
        fwd1.append(gather_copy(2, n, far * tiles + source(d), sib, spread))
        fwd1[-1].start()
        add_member(far, source(d))
    for n, d in enumerate(arrive):
        core1[n].wait_recv()
        add_member(sib, source(d))
    for n, d in enumerate(arrive):
        fwd1[n].wait_recv()
        add_member(diag, source(d))

    norm = 1.0 / math.sqrt(members)
    adj[...] = sea[...] * ((inc[...] * norm * obs_acc[0] - obs_acc[1]) * norm)

    def partial(slot, u):
        k, c = u // blocks, lax.rem(u, blocks)
        return member_block(pert, slot * own + k, c).astype(F32) * at_block(adj, c)

    core2, near2, far2 = [], [], []
    for d in order:
        u = lax.rem(h + d, tiles)
        stage_c[u] = partial(diag, u).astype(BF16)
        core2.append(to_slot(red_ss, red_rs, 0, d, stage_c.at[u], recv_c.at[u], sib))
        core2[-1].start()
    for d in order:
        u = lax.rem(h + d, tiles)
        stage_c[tiles + u] = partial(sib, u).astype(BF16)
        near2.append(
            to_slot(red_ss, red_rs, 1, d, stage_c.at[tiles + u], recv_c.at[tiles + u], sib)
        )
        near2[-1].start()
    for n, d in enumerate(order):
        u = lax.rem(h + d, tiles)
        core2[n].wait_recv()
        stage_x[u] = (partial(far, u) + recv_c[u].astype(F32)).astype(BF16)
        far2.append(to_slot(red_ss, red_rs, 2, d, stage_x.at[u], recv_x.at[u], far))
        far2[-1].start()
    third = []
    for n, d in enumerate(order):
        u = lax.rem(h + d, tiles)
        near2[n].wait_recv()
        far2[n].wait_recv()
        total = partial(s, u) + recv_c[tiles + u].astype(F32) + recv_x[u].astype(F32)
        if d == 0:
            recv_d[h] = total.astype(BF16)
        else:
            stage_d[u] = total.astype(BF16)
            copy = to_tile(2, d, stage_d.at[u], recv_d.at[h])
            copy.start()
            third.append(copy)

    for d in arrive:
        if d > 0:
            third[place[d]].wait_recv()
        deep[source(d)] = dot(kz[...], recv_d[source(d)]).astype(BF16)
    filter_y(ky, deep, stage_e)
    fourth = []
    for d in order:
        u = lax.rem(h + d, tiles)
        if d == 0:
            recv_e[h] = stage_e[h]
        else:
            copy = to_tile(3, d, stage_e.at[u], recv_e.at[h])
            copy.start()
            fourth.append(copy)

    if blocks > 1:
        for copy in fourth:
            copy.wait_recv()
    core3, far3, fwd3 = [], [], []
    for n in range(own):
        if blocks == 1:
            if n > 0:
                fourth[n - 1].wait_recv()
            k = source(arrive[n])
            field = recv_e[k]
        else:
            k = n
            field = jnp.concatenate([recv_e[n * blocks + c] for c in range(blocks)], axis=1)
        field = (field.astype(F32) * sea[...]).astype(BF16)
        m = s * own + k
        out[m] = (
            control[k].astype(F32) + weight[...] * dot(field, inv_x[...], 1, 1)
        ).astype(BF16)
        far3.append(gather_copy(4, n, m, far, out))
        far3[-1].start()
        core3.append(gather_copy(3, n, m, sib, out))
        core3[-1].start()
    for n in range(own):
        k = source(arrive[n]) if blocks == 1 else n
        far3[n].wait_recv()
        fwd3.append(gather_copy(5, n, far * own + k, sib, out))
        fwd3[-1].start()
    for n in range(own):
        core3[n].wait_recv()
        fwd3[n].wait_recv()
    for copy in (
        first + second + third + fourth + core1 + far1 + fwd1 + core2 + near2 + far2 + core3
        + far3 + fwd3
    ):
        copy.wait_send()


def store_kernel(src, dst, sem):
    copy = pltpu.make_async_copy(src, dst, sem)
    copy.start()
    copy.wait()


def per_device(
    slots,
    tiles,
    control,
    land_mask,
    tile_id,
    tile_scale,
    inverse_x,
    inverse_y,
    inverse_z,
    perturbations,
    obs_cell,
    obs_value,
    obs_weight,
):
    members, levels, rows, cols = control.shape
    depth = levels * rows
    blocks = cols // LANES
    assert slots == 4 and cols % LANES == 0 and cols & (cols - 1) == 0
    assert members // slots * blocks == tiles and depth % GROUP == 0 and 4 % rows == 0
    unit = (depth, LANES)
    whole = pl.BlockSpec(memory_space=pl.ANY)
    vmem = pl.BlockSpec(memory_space=pltpu.VMEM)
    gradient = pl.pallas_call(
        functools.partial(kernel, slots, tiles, rows),
        out_shape=jax.ShapeDtypeStruct((members, depth, cols), BF16),
        in_specs=[whole] + [vmem] * 6 + [whole] + [vmem] * 3,
        out_specs=vmem,
        scratch_shapes=[
            pltpu.VMEM((members // slots, depth, cols), BF16),
            pltpu.VMEM((members, depth, cols), BF16),
            pltpu.VMEM((depth, cols), F32),
            pltpu.VMEM((depth, cols), F32),
            pltpu.VMEM((tiles * GROUP, tiles * GROUP), BF16),
            pltpu.VMEM((tiles * GROUP, tiles * GROUP), BF16),
            pltpu.VMEM((depth, depth), BF16),
            pltpu.VMEM((depth, depth), BF16),
            pltpu.VMEM((2, depth, cols), F32),
            pltpu.VMEM((depth, cols), F32),
            pltpu.VMEM((depth, cols), F32),
            pltpu.VMEM((tiles,) + unit, BF16),
            pltpu.VMEM((tiles,) + unit, BF16),
            pltpu.VMEM((tiles,) + unit, BF16),
            pltpu.VMEM((tiles,) + unit, BF16),
            pltpu.VMEM((slots * tiles,) + unit, BF16),
            pltpu.VMEM((2 * tiles,) + unit, BF16),
            pltpu.VMEM((2 * tiles,) + unit, BF16),
            pltpu.VMEM((tiles,) + unit, BF16),
            pltpu.VMEM((tiles,) + unit, BF16),
            pltpu.VMEM((tiles,) + unit, BF16),
            pltpu.VMEM((tiles,) + unit, BF16),
            pltpu.VMEM((tiles,) + unit, BF16),
            pltpu.VMEM((tiles,) + unit, BF16),
            pltpu.VMEM((tiles,) + unit, BF16),
            pltpu.SemaphoreType.DMA((4, tiles)),
            pltpu.SemaphoreType.DMA((4, tiles)),
            pltpu.SemaphoreType.DMA((6, tiles)),
            pltpu.SemaphoreType.DMA((6, tiles)),
            pltpu.SemaphoreType.DMA((3, tiles)),
            pltpu.SemaphoreType.DMA((3, tiles)),
            pltpu.SemaphoreType.DMA((2,)),
        ],
        compiler_params=pltpu.CompilerParams(
            collective_id=0, has_side_effects=True, vmem_limit_bytes=56 * 1024 * 1024
        ),
    )(
        control.reshape(members, depth, cols),
        land_mask.reshape(depth, cols),
        tile_id,
        tile_scale,
        inverse_x,
        inverse_y,
        inverse_z,
        perturbations.reshape(members, depth, cols),
        obs_cell,
        obs_value,
        obs_weight,
    )
    gradient = pl.pallas_call(
        store_kernel,
        out_shape=jax.ShapeDtypeStruct(gradient.shape, BF16),
        in_specs=[whole],
        out_specs=whole,
        scratch_shapes=[pltpu.SemaphoreType.DMA],
    )(gradient)
    return gradient.reshape(members, levels, rows, cols)


def solution(mesh):
    return jax.shard_map(
        functools.partial(per_device, mesh.shape["slot"], mesh.shape["horiz"]),
        mesh=mesh,
        in_specs=(
            P(None, None, "horiz", None),
            P(None, "horiz", None),
            P(),
            P(),
            P(),
            P(),
            P(),
            P("slot", None, None, "horiz", None),
            P("slot", "horiz"),
            P("slot", "horiz"),
            P("slot", "horiz"),
        ),
        out_specs=P(None, None, "horiz", None),
        check_vma=False,
    )
```

```python
import functools
import math

import jax
import jax.numpy as jnp
from jax import lax
from jax.experimental import pallas as pl
from jax.experimental.pallas import tpu as pltpu
from jax.sharding import PartitionSpec as P

LANES = 128
GROUP = 16
F32 = jnp.float32
BF16 = jnp.bfloat16
MESH = pl.DeviceIdType.MESH


def dot(a, b, ca=1, cb=0, precision=None):
    return lax.dot_general(
        a, b, (((ca,), (cb,)), ((), ())), preferred_element_type=F32, precision=precision
    )


def iota(shape, dim):
    return lax.broadcasted_iota(jnp.int32, shape, dim)


def spread_matrix(shape, index):
    return jnp.where(index == iota(shape, 1), 1.0, 0.0).astype(BF16)


def kernel(
    slots,
    tiles,
    rows,
    groups,
    control_hbm,
    land,
    tile_id,
    tile_scale,
    inv_x,
    inv_y,
    inv_z,
    pert_hbm,
    cells,
    values,
    weights,
    out,
    control,
    pert,
    sea,
    weight,
    ky,
    ky_t,
    kz,
    kz_t,
    obs_acc,
    inc,
    adj,
    send_a,
    recv_a,
    send_b,
    spread,
    stage_c,
    recv_c,
    stage_x,
    recv_x,
    stage_d,
    recv_d,
    deep,
    stage_e,
    recv_e,
    tile_ss,
    tile_rs,
    slot_ss,
    slot_rs,
    last_ss,
    last_rs,
    load_sem,
):
    members, depth, cols = control_hbm.shape
    own = members // slots
    blocks = cols // LANES
    levels = depth // rows
    part = depth // groups
    s = lax.axis_index("slot")
    h = lax.axis_index("horiz")
    sib = s + 1 - 2 * lax.rem(s, 2)
    far = s + 2 - 4 * (s // 2)
    diag = sib + 2 - 4 * (sib // 2)

    barrier = pltpu.get_barrier_semaphore()
    for d in range(1, tiles):
        pl.semaphore_signal(
            barrier, inc=1, device_id={"horiz": lax.rem(h + d, tiles)}, device_id_type=MESH
        )
    for peer in (sib, far):
        pl.semaphore_signal(barrier, inc=1, device_id={"slot": peer}, device_id_type=MESH)

    load_control = pltpu.make_async_copy(
        control_hbm.at[pl.ds(s * own, own)], control, load_sem.at[0]
    )
    load_pert = pltpu.make_async_copy(pert_hbm, pert, load_sem.at[1])
    load_control.start()
    load_pert.start()

    def target(n):
        return lax.rem(h + 1 + n, tiles)

    def source(n):
        return lax.rem(h - 1 - n + 2 * tiles, tiles)

    def each(count, body):
        if count <= 8:
            for n in range(count):
                body(n)
        else:
            lax.fori_loop(0, count, lambda n, carry: (body(n), carry)[1], 0)

    def at_block(ref, c, where=slice(None)):
        if blocks == 1:
            return ref[where]
        return ref[where, pl.ds(pl.multiple_of(c * LANES, LANES), LANES)]

    def pert_rows(slot, unit, where):
        k, c = unit // blocks, lax.rem(unit, blocks)
        if blocks == 1:
            return pert[slot * own + k, where].astype(F32)
        lanes = pl.ds(pl.multiple_of(c * LANES, LANES), LANES)
        return pert[slot * own + k, where, lanes].astype(F32)

    def rows_of(g):
        return slice(g * part, (g + 1) * part)

    def to_tile(phase, g, n, src, dst):
        return pltpu.make_async_remote_copy(
            src_ref=src,
            dst_ref=dst,
            send_sem=tile_ss.at[phase, g, n],
            recv_sem=tile_rs.at[phase, g, n],
            device_id={"horiz": target(n)},
            device_id_type=MESH,
        )

    def to_slot(phase, g, src, dst, peer):
        return pltpu.make_async_remote_copy(
            src_ref=src,
            dst_ref=dst,
            send_sem=slot_ss.at[phase, g],
            recv_sem=slot_rs.at[phase, g],
            device_id={"slot": peer},
            device_id_type=MESH,
        )

    def copy_a(g, n):
        return to_tile(0, g, n, send_a.at[g, n], recv_a.at[g, h])

    def copy_b(g, n):
        return to_tile(1, g, n, send_b.at[g, target(n)], spread.at[g, s, n])

    def copy_d(g, n):
        return to_tile(2, g, n, stage_d.at[g, n], recv_d.at[g, h])

    def copy_e(n):
        return to_tile(3, 0, n, stage_e.at[target(n)], recv_e.at[n])

    def copy_far(g):
        return to_slot(0, g, spread.at[g, s], spread.at[g, s], far)

    def copy_core(g):
        return to_slot(1, g, spread.at[g, s], spread.at[g, s], sib)

    def copy_on(g):
        return to_slot(2, g, spread.at[g, far], spread.at[g, far], sib)

    def copy_sum(g, n):
        return to_slot(3 + n, g, stage_c.at[g, n], recv_c.at[g, n], sib)

    def copy_x(g):
        return to_slot(5, g, stage_x.at[g], recv_x.at[g], far)

    def copy_last(phase, n, m, peer):
        return pltpu.make_async_remote_copy(
            src_ref=out.at[m],
            dst_ref=out.at[m],
            send_sem=last_ss.at[phase, n],
            recv_sem=last_rs.at[phase, n],
            device_id={"slot": peer},
            device_id_type=MESH,
        )

    others = tiles - 1

    region = tile_id[pl.ds(h * rows // 4, 1), :].astype(F32).astype(BF16)
    blocks_x = tile_id.shape[1]
    widen = jnp.where(iota((blocks_x, cols), 1) // 4 == iota((blocks_x, cols), 0), 1.0, 0.0)
    region_x = dot(region, widen.astype(BF16))
    regions = tile_scale.shape[0]
    onehot = jnp.where(iota((regions, cols), 0).astype(F32) == region_x, 1.0, 0.0)
    to_level = spread_matrix((depth, levels), iota((depth, levels), 0) // rows)
    scale_rows = dot(
        to_level.astype(F32), tile_scale[...], 1, 1, precision=lax.Precision.HIGHEST
    )
    sea[...] = land[...].astype(F32)
    weight[...] = sea[...] * dot(scale_rows, onehot, precision=lax.Precision.HIGHEST)

    same = lax.rem(iota((depth, depth), 0), rows) == lax.rem(iota((depth, depth), 1), rows)
    half = dot(to_level, inv_z[...], 1, 1).astype(BF16)
    kz_t[...] = jnp.where(same, dot(half, to_level, 1, 1), 0.0).astype(BF16)

    load_control.wait()

    def forward(n):
        u = target(n)
        k, c = u // blocks, lax.rem(u, blocks)
        masked = (weight[...] * control[k].astype(F32)).astype(BF16)
        along = (at_block(sea, c) * dot(masked, at_block(inv_x, c))).astype(BF16)
        return dot(kz_t[...], along).astype(BF16).reshape(groups, part, LANES)

    pl.semaphore_wait(barrier, tiles - 1 + 2)

    def send_first(n):
        send_a[:, n] = forward(n)
        copy_a(0, n).start()

    each(others, send_first)
    for g in range(1, groups):
        each(others, lambda n: copy_a(g, n).start())
    mine = forward(others)
    for g in range(groups):
        recv_a[g, h] = mine[g]

    wide = tiles * GROUP
    side = tiles * rows
    pos = iota((wide, side), 0)
    pick_y = spread_matrix((wide, side), pos // GROUP * rows + lax.rem(pos, rows))
    row_i, col_i = iota((wide, wide), 0), iota((wide, wide), 1)
    same_level = lax.rem(row_i, GROUP) // rows == lax.rem(col_i, GROUP) // rows
    half = dot(pick_y, inv_y[...], 1, 1).astype(BF16)
    ky_t[...] = jnp.where(same_level, dot(half, pick_y, 1, 1), 0.0).astype(BF16)

    def filter_y(matrix, src, dst, g):
        for i in range(part // GROUP):
            some = src[g, :, i * GROUP : (i + 1) * GROUP, :].reshape(wide, LANES)
            dst[g, :, i * GROUP : (i + 1) * GROUP, :] = (
                dot(matrix[...], some).astype(BF16).reshape(tiles, GROUP, LANES)
            )

    count = cells.shape[1]
    step = min(1024, count)
    chunks = count // step
    shift = cols.bit_length() - 1
    obs_acc[...] = jnp.zeros_like(obs_acc)

    def observe(i, carry):
        where = pl.ds(pl.multiple_of(i * step, step), step)
        cell, w = cells[:, where], weights[:, where]
        wv = w * values[:, where]
        w_hi = w.astype(BF16).astype(F32)
        v_hi = wv.astype(BF16).astype(F32)
        on_row = jnp.where(iota((depth, step), 0) == (cell >> shift), 1.0, 0.0).astype(BF16)
        on_col = iota((cols, step), 0) == (cell & (cols - 1))
        parts = [
            jnp.where(on_col, x, 0.0).astype(BF16) for x in (w_hi, w - w_hi, v_hi, wv - v_hi)
        ]
        for n, x in enumerate(parts):
            obs_acc[n // 2] += dot(on_row, x, 1, 1)
        return carry

    ahead = max(chunks - groups, 0)
    lax.fori_loop(0, ahead, observe, 0)
    inc[...] = jnp.zeros_like(inc)

    for g in range(groups):
        each(others, lambda n: copy_a(g, n).wait_recv())
        filter_y(ky_t, recv_a, send_b, g)
        each(others, lambda n: copy_b(g, n).start())
        spread[g, s, others] = send_b[g, h]
        begin = min(ahead + g, chunks)
        lax.fori_loop(begin, chunks if g == groups - 1 else min(begin + 1, chunks), observe, 0)
    load_pert.wait()

    norm = 1.0 / math.sqrt(members)

    def add_slot(g, slot):
        where = rows_of(g)

        def one(n):
            unit = source(n)
            term = pert_rows(slot, unit, where) * spread[g, slot, n].astype(F32)
            if blocks == 1:
                inc[where] += term
            else:
                c = lax.rem(unit, blocks)
                inc[where, pl.ds(pl.multiple_of(c * LANES, LANES), LANES)] += term

        each(tiles, one)

    def partial(g, slot, n):
        u = target(n)
        return pert_rows(slot, u, rows_of(g)) * at_block(adj, lax.rem(u, blocks), rows_of(g))

    def gather(g):
        each(others, lambda n: copy_b(g, n).wait_recv())
        copy_far(g).start()
        copy_core(g).start()
        add_slot(g, s)

    def pass_on(g):
        copy_far(g).wait_recv()
        copy_on(g).start()
        add_slot(g, far)
        copy_core(g).wait_recv()
        add_slot(g, sib)

    def observed(g):
        copy_on(g).wait_recv()
        add_slot(g, diag)
        where = rows_of(g)
        adj[where] = sea[where] * (
            (inc[where] * norm * obs_acc[0, where] - obs_acc[1, where]) * norm
        )
        for i, slot in enumerate((diag, sib)):

            def fill(n):
                stage_c[g, i, n] = partial(g, slot, n).astype(BF16)

            each(tiles, fill)
            copy_sum(g, i).start()

    def between_chips(g):
        copy_sum(g, 0).wait_recv()

        def fill(n):
            stage_x[g, n] = (partial(g, far, n) + recv_c[g, 0, n].astype(F32)).astype(BF16)

        each(tiles, fill)
        copy_x(g).start()

    def exchange(g):
        copy_sum(g, 1).wait_recv()
        copy_x(g).wait_recv()

        def total(n):
            value = partial(g, s, n) + recv_c[g, 1, n].astype(F32) + recv_x[g, n].astype(F32)
            return value.astype(BF16)

        def fill(n):
            stage_d[g, n] = total(n)
            copy_d(g, n).start()

        each(others, fill)
        recv_d[g, h] = total(others)

    stages = ((0, gather), (2, pass_on), (3, observed), (4, between_chips), (5, exchange))
    for t in range(groups + 5):
        for delay, stage in stages:
            if 0 <= t - delay < groups:
                stage(t - delay)
        if t == groups:
            half = dot(pick_y, inv_y[...]).astype(BF16)
            ky[...] = jnp.where(same_level, dot(half, pick_y, 1, 1), 0.0).astype(BF16)
            half = dot(to_level, inv_z[...]).astype(BF16)
            kz[...] = jnp.where(same, dot(half, to_level, 1, 1), 0.0).astype(BF16)

    for g in range(groups):
        each(others, lambda n: copy_a(g, n).wait_send())
        each(others, lambda n: copy_b(g, n).wait_send())
        for copy in (copy_far, copy_core, copy_on):
            copy(g).wait_send()
    for g in range(groups):
        each(others, lambda n: copy_d(g, n).wait_recv())
        filter_y(ky, recv_d, deep, g)

    def adjoint(u):
        return dot(kz[...], deep[:, u].reshape(depth, LANES)).astype(BF16)

    def send_last(n):
        stage_e[target(n)] = adjoint(target(n))
        copy_e(n).start()

    each(others, send_last)
    recv_e[others] = adjoint(h)

    def member(n):
        if blocks > 1:
            return n
        return source(n)

    if blocks > 1:
        each(others, lambda n: copy_e(n).wait_recv())
    turns = [own - 1] + list(range(own - 1))
    for n in turns:
        k = member(n)
        if blocks == 1:
            if n < others:
                copy_e(n).wait_recv()
            field = recv_e[n]
        else:
            field = jnp.concatenate(
                [recv_e[source(n * blocks + c)] for c in range(blocks)], axis=1
            )
        field = (field.astype(F32) * sea[...]).astype(BF16)
        m = s * own + k
        out[m] = (
            control[k].astype(F32) + weight[...] * dot(field, inv_x[...], 1, 1)
        ).astype(BF16)
        copy_last(0, n, m, far).start()
        copy_last(1, n, m, sib).start()
    for n in turns:
        copy_last(0, n, s * own + member(n), far).wait_recv()
        copy_last(2, n, far * own + member(n), sib).start()
    for g in range(groups):
        each(others, lambda n: copy_d(g, n).wait_send())
        copy_sum(g, 0).wait_send()
        copy_sum(g, 1).wait_send()
        copy_x(g).wait_send()
    each(others, lambda n: copy_e(n).wait_send())
    for n in turns:
        for phase, slot, peer in ((0, s, far), (1, s, sib), (2, far, sib)):
            copy = copy_last(phase, n, slot * own + member(n), peer)
            copy.wait_send()
            if phase > 0:
                copy.wait_recv()


def store_kernel(src, dst):
    dst[...] = src[...]


def per_device(
    slots,
    tiles,
    control,
    land_mask,
    tile_id,
    tile_scale,
    inverse_x,
    inverse_y,
    inverse_z,
    perturbations,
    obs_cell,
    obs_value,
    obs_weight,
):
    members, levels, rows, cols = control.shape
    depth = levels * rows
    blocks = cols // LANES
    assert slots == 4 and cols % LANES == 0 and cols & (cols - 1) == 0
    assert members // slots * blocks == tiles and depth % GROUP == 0 and 4 % rows == 0
    groups = next(n for n in (5, 2, 1) if depth % (n * GROUP) == 0)
    piece = (depth // groups, LANES)
    units = (groups, tiles) + piece
    whole = pl.BlockSpec(memory_space=pl.ANY)
    vmem = pl.BlockSpec(memory_space=pltpu.VMEM)
    gradient = pl.pallas_call(
        functools.partial(kernel, slots, tiles, rows, groups),
        out_shape=jax.ShapeDtypeStruct((members, depth, cols), BF16),
        in_specs=[whole] + [vmem] * 6 + [whole] + [vmem] * 3,
        out_specs=vmem,
        scratch_shapes=[
            pltpu.VMEM((members // slots, depth, cols), BF16),
            pltpu.VMEM((members, depth, cols), BF16),
            pltpu.VMEM((depth, cols), F32),
            pltpu.VMEM((depth, cols), F32),
            pltpu.VMEM((tiles * GROUP, tiles * GROUP), BF16),
            pltpu.VMEM((tiles * GROUP, tiles * GROUP), BF16),
            pltpu.VMEM((depth, depth), BF16),
            pltpu.VMEM((depth, depth), BF16),
            pltpu.VMEM((2, depth, cols), F32),
            pltpu.VMEM((depth, cols), F32),
            pltpu.VMEM((depth, cols), F32),
            pltpu.VMEM(units, BF16),
            pltpu.VMEM(units, BF16),
            pltpu.VMEM(units, BF16),
            pltpu.VMEM((groups, slots, tiles) + piece, BF16),
            pltpu.VMEM((groups, 2, tiles) + piece, BF16),
            pltpu.VMEM((groups, 2, tiles) + piece, BF16),
            pltpu.VMEM(units, BF16),
            pltpu.VMEM(units, BF16),
            pltpu.VMEM(units, BF16),
            pltpu.VMEM(units, BF16),
            pltpu.VMEM(units, BF16),
            pltpu.VMEM((tiles, depth, LANES), BF16),
            pltpu.VMEM((tiles, depth, LANES), BF16),
            pltpu.SemaphoreType.DMA((4, groups, tiles)),
            pltpu.SemaphoreType.DMA((4, groups, tiles)),
            pltpu.SemaphoreType.DMA((6, groups)),
            pltpu.SemaphoreType.DMA((6, groups)),
            pltpu.SemaphoreType.DMA((3, members // slots)),
            pltpu.SemaphoreType.DMA((3, members // slots)),
            pltpu.SemaphoreType.DMA((2,)),
        ],
        compiler_params=pltpu.CompilerParams(
            collective_id=0, has_side_effects=True, vmem_limit_bytes=56 * 1024 * 1024
        ),
    )(
        control.reshape(members, depth, cols),
        land_mask.reshape(depth, cols),
        tile_id,
        tile_scale,
        inverse_x,
        inverse_y,
        inverse_z,
        perturbations.reshape(members, depth, cols),
        obs_cell,
        obs_value,
        obs_weight,
    )
    block = pl.BlockSpec((members // 4, depth, cols), lambda i: (i, 0, 0))
    gradient = pl.pallas_call(
        store_kernel,
        out_shape=jax.ShapeDtypeStruct(gradient.shape, BF16),
        grid=(4,),
        in_specs=[block],
        out_specs=block,
    )(gradient)
    return gradient.reshape(members, levels, rows, cols)


def solution(mesh):
    return jax.shard_map(
        functools.partial(per_device, mesh.shape["slot"], mesh.shape["horiz"]),
        mesh=mesh,
        in_specs=(
            P(None, None, "horiz", None),
            P(None, "horiz", None),
            P(),
            P(),
            P(),
            P(),
            P(),
            P("slot", None, None, "horiz", None),
            P("slot", "horiz"),
            P("slot", "horiz"),
            P("slot", "horiz"),
        ),
        out_specs=P(None, None, "horiz", None),
        check_vma=False,
    )
```

```python
import functools
import math

import jax
import jax.numpy as jnp
from jax import lax
from jax.experimental import pallas as pl
from jax.experimental.pallas import tpu as pltpu
from jax.sharding import PartitionSpec as P

LANES = 128
GROUP = 16
F32 = jnp.float32
BF16 = jnp.bfloat16
MESH = pl.DeviceIdType.MESH


def dot(a, b, ca=1, cb=0, precision=None):
    return lax.dot_general(
        a, b, (((ca,), (cb,)), ((), ())), preferred_element_type=F32, precision=precision
    )


def iota(shape, dim):
    return lax.broadcasted_iota(jnp.int32, shape, dim)


def spread_matrix(shape, index):
    return jnp.where(index == iota(shape, 1), 1.0, 0.0).astype(BF16)


def kernel(
    slots,
    tiles,
    rows,
    groups,
    control_hbm,
    land,
    tile_id,
    tile_scale,
    inv_x,
    inv_y,
    inv_z,
    pert_hbm,
    cells,
    values,
    weights,
    out,
    control,
    pert,
    sea,
    weight,
    ky,
    ky_t,
    kz,
    kz_t,
    obs_acc,
    cell_sum,
    inc,
    adj,
    send_a,
    recv_a,
    send_b,
    spread,
    stage_c,
    recv_c,
    stage_x,
    recv_x,
    stage_d,
    recv_d,
    deep,
    stage_e,
    recv_e,
    tile_ss,
    tile_rs,
    slot_ss,
    slot_rs,
    last_ss,
    last_rs,
    load_sem,
):
    members, depth, cols = control_hbm.shape
    own = members // slots
    blocks = cols // LANES
    levels = depth // rows
    part = depth // groups
    s = lax.axis_index("slot")
    h = lax.axis_index("horiz")
    sib = s + 1 - 2 * lax.rem(s, 2)
    far = s + 2 - 4 * (s // 2)
    diag = sib + 2 - 4 * (sib // 2)

    barrier = pltpu.get_barrier_semaphore()
    for d in range(1, tiles):
        pl.semaphore_signal(
            barrier, inc=1, device_id={"horiz": lax.rem(h + d, tiles)}, device_id_type=MESH
        )
    for peer in (sib, far):
        pl.semaphore_signal(barrier, inc=1, device_id={"slot": peer}, device_id_type=MESH)

    load_control = pltpu.make_async_copy(
        control_hbm.at[pl.ds(s * own, own)], control, load_sem.at[0]
    )
    load_pert = pltpu.make_async_copy(pert_hbm, pert, load_sem.at[1])
    load_control.start()
    load_pert.start()

    def target(n):
        return lax.rem(h + 1 + n, tiles)

    def source(n):
        return lax.rem(h - 1 - n + 2 * tiles, tiles)

    def each(count, body):
        if count <= 8:
            for n in range(count):
                body(n)
        else:
            lax.fori_loop(0, count, lambda n, carry: (body(n), carry)[1], 0)

    def at_block(ref, c, where=slice(None)):
        if blocks == 1:
            return ref[where]
        return ref[where, pl.ds(pl.multiple_of(c * LANES, LANES), LANES)]

    def pert_rows(slot, unit, where):
        k, c = unit // blocks, lax.rem(unit, blocks)
        if blocks == 1:
            return pert[slot * own + k, where].astype(F32)
        lanes = pl.ds(pl.multiple_of(c * LANES, LANES), LANES)
        return pert[slot * own + k, where, lanes].astype(F32)

    def rows_of(g):
        return slice(g * part, (g + 1) * part)

    def to_tile(phase, g, n, src, dst):
        return pltpu.make_async_remote_copy(
            src_ref=src,
            dst_ref=dst,
            send_sem=tile_ss.at[phase, g, n],
            recv_sem=tile_rs.at[phase, g, n],
            device_id={"horiz": target(n)},
            device_id_type=MESH,
        )

    def to_slot(phase, g, src, dst, peer):
        return pltpu.make_async_remote_copy(
            src_ref=src,
            dst_ref=dst,
            send_sem=slot_ss.at[phase, g],
            recv_sem=slot_rs.at[phase, g],
            device_id={"slot": peer},
            device_id_type=MESH,
        )

    def copy_a(g, n):
        return to_tile(0, g, n, send_a.at[g, n], recv_a.at[g, h])

    def copy_b(g, n):
        return to_tile(1, g, n, send_b.at[g, target(n)], spread.at[g, s, n])

    def copy_d(g, n):
        return to_tile(2, g, n, stage_d.at[g, n], recv_d.at[g, h])

    def copy_e(n):
        return to_tile(3, 0, n, stage_e.at[target(n)], recv_e.at[n])

    def copy_far(g):
        return to_slot(0, g, spread.at[g, s], spread.at[g, s], far)

    def copy_core(g):
        return to_slot(1, g, spread.at[g, s], spread.at[g, s], sib)

    def copy_on(g):
        return to_slot(2, g, spread.at[g, far], spread.at[g, far], sib)

    def copy_sum(g, n):
        return to_slot(3 + n, g, stage_c.at[g, n], recv_c.at[g, n], sib)

    def copy_x(g):
        return to_slot(5, g, stage_x.at[g], recv_x.at[g], far)

    def copy_last(phase, n, m, peer):
        return pltpu.make_async_remote_copy(
            src_ref=out.at[m],
            dst_ref=out.at[m],
            send_sem=last_ss.at[phase, n],
            recv_sem=last_rs.at[phase, n],
            device_id={"slot": peer},
            device_id_type=MESH,
        )

    others = tiles - 1

    region = tile_id[pl.ds(h * rows // 4, 1), :].astype(F32).astype(BF16)
    blocks_x = tile_id.shape[1]
    widen = jnp.where(iota((blocks_x, cols), 1) // 4 == iota((blocks_x, cols), 0), 1.0, 0.0)
    region_x = dot(region, widen.astype(BF16))
    regions = tile_scale.shape[0]
    onehot = jnp.where(iota((regions, cols), 0).astype(F32) == region_x, 1.0, 0.0)
    to_level = spread_matrix((depth, levels), iota((depth, levels), 0) // rows)
    scale_rows = dot(
        to_level.astype(F32), tile_scale[...], 1, 1, precision=lax.Precision.HIGHEST
    )
    sea[...] = land[...].astype(F32)
    weight[...] = sea[...] * dot(scale_rows, onehot, precision=lax.Precision.HIGHEST)

    same = lax.rem(iota((depth, depth), 0), rows) == lax.rem(iota((depth, depth), 1), rows)
    half = dot(to_level, inv_z[...], 1, 1).astype(BF16)
    kz_t[...] = jnp.where(same, dot(half, to_level, 1, 1), 0.0).astype(BF16)

    load_control.wait()

    def forward(n):
        u = target(n)
        k, c = u // blocks, lax.rem(u, blocks)
        masked = (weight[...] * control[k].astype(F32)).astype(BF16)
        along = (at_block(sea, c) * dot(masked, at_block(inv_x, c))).astype(BF16)
        return dot(kz_t[...], along).astype(BF16).reshape(groups, part, LANES)

    pl.semaphore_wait(barrier, tiles - 1 + 2)

    def send_first(n):
        send_a[:, n] = forward(n)
        copy_a(0, n).start()

    each(others, send_first)
    for g in range(1, groups):
        each(others, lambda n: copy_a(g, n).start())
    mine = forward(others)
    for g in range(groups):
        recv_a[g, h] = mine[g]

    wide = tiles * GROUP
    side = tiles * rows
    pos = iota((wide, side), 0)
    pick_y = spread_matrix((wide, side), pos // GROUP * rows + lax.rem(pos, rows))
    row_i, col_i = iota((wide, wide), 0), iota((wide, wide), 1)
    same_level = lax.rem(row_i, GROUP) // rows == lax.rem(col_i, GROUP) // rows
    half = dot(pick_y, inv_y[...], 1, 1).astype(BF16)
    ky_t[...] = jnp.where(same_level, dot(half, pick_y, 1, 1), 0.0).astype(BF16)

    def filter_y(matrix, src, dst, g):
        for i in range(part // GROUP):
            some = src[g, :, i * GROUP : (i + 1) * GROUP, :].reshape(wide, LANES)
            dst[g, :, i * GROUP : (i + 1) * GROUP, :] = (
                dot(matrix[...], some).astype(BF16).reshape(tiles, GROUP, LANES)
            )

    count = cells.shape[1]
    step = min(1024, count)
    chunks = count // step
    shift = cols.bit_length() - 1
    obs_acc[...] = jnp.zeros_like(obs_acc)

    def observe(i, carry):
        where = pl.ds(pl.multiple_of(i * step, step), step)
        cell, w = cells[:, where], weights[:, where]
        wv = w * values[:, where]
        w_hi = w.astype(BF16).astype(F32)
        v_hi = wv.astype(BF16).astype(F32)
        on_row = jnp.where(iota((depth, step), 0) == (cell >> shift), 1.0, 0.0).astype(BF16)
        on_col = iota((cols, step), 0) == (cell & (cols - 1))
        parts = [
            jnp.where(on_col, x, 0.0).astype(BF16) for x in (w_hi, w - w_hi, v_hi, wv - v_hi)
        ]
        obs_acc[...] += dot(jnp.concatenate(parts, axis=0), on_row, 1, 1)
        return carry

    ahead = chunks // 2
    lax.fori_loop(0, ahead, observe, 0)
    inc[...] = jnp.zeros_like(inc)

    for g in range(groups):
        each(others, lambda n: copy_a(g, n).wait_recv())
        filter_y(ky_t, recv_a, send_b, g)
        each(others, lambda n: copy_b(g, n).start())
        spread[g, s, others] = send_b[g, h]
    lax.fori_loop(ahead, chunks, observe, 0)
    for i in range(2):
        both = obs_acc[2 * i * cols : (2 * i + 1) * cols]
        both += obs_acc[(2 * i + 1) * cols : (2 * i + 2) * cols]
        cell_sum[i] = both.T
    load_pert.wait()

    norm = 1.0 / math.sqrt(members)

    def add_slot(g, slot):
        where = rows_of(g)

        def one(n):
            unit = source(n)
            term = pert_rows(slot, unit, where) * spread[g, slot, n].astype(F32)
            if blocks == 1:
                inc[where] += term
            else:
                c = lax.rem(unit, blocks)
                inc[where, pl.ds(pl.multiple_of(c * LANES, LANES), LANES)] += term

        each(tiles, one)

    def partial(g, slot, n):
        u = target(n)
        return pert_rows(slot, u, rows_of(g)) * at_block(adj, lax.rem(u, blocks), rows_of(g))

    def gather(g):
        each(others, lambda n: copy_b(g, n).wait_recv())
        copy_far(g).start()
        copy_core(g).start()
        add_slot(g, s)

    def pass_on(g):
        copy_far(g).wait_recv()
        copy_on(g).start()
        add_slot(g, far)
        copy_core(g).wait_recv()
        add_slot(g, sib)

    def observed(g):
        copy_on(g).wait_recv()
        add_slot(g, diag)
        where = rows_of(g)
        adj[where] = sea[where] * (
            (inc[where] * norm * cell_sum[0, where] - cell_sum[1, where]) * norm
        )
        for i, slot in enumerate((diag, sib)):

            def fill(n):
                stage_c[g, i, n] = partial(g, slot, n).astype(BF16)

            each(tiles, fill)
            copy_sum(g, i).start()

    def between_chips(g):
        copy_sum(g, 0).wait_recv()

        def fill(n):
            stage_x[g, n] = (partial(g, far, n) + recv_c[g, 0, n].astype(F32)).astype(BF16)

        each(tiles, fill)
        copy_x(g).start()

    def exchange(g):
        copy_sum(g, 1).wait_recv()
        copy_x(g).wait_recv()

        def total(n):
            value = partial(g, s, n) + recv_c[g, 1, n].astype(F32) + recv_x[g, n].astype(F32)
            return value.astype(BF16)

        def fill(n):
            stage_d[g, n] = total(n)
            copy_d(g, n).start()

        each(others, fill)
        recv_d[g, h] = total(others)

    stages = ((0, gather), (2, pass_on), (3, observed), (4, between_chips), (5, exchange))
    for t in range(groups + 5):
        for delay, stage in stages:
            if 0 <= t - delay < groups:
                stage(t - delay)
        if t == groups:
            half = dot(pick_y, inv_y[...]).astype(BF16)
            ky[...] = jnp.where(same_level, dot(half, pick_y, 1, 1), 0.0).astype(BF16)
            half = dot(to_level, inv_z[...]).astype(BF16)
            kz[...] = jnp.where(same, dot(half, to_level, 1, 1), 0.0).astype(BF16)

    for g in range(groups):
        each(others, lambda n: copy_a(g, n).wait_send())
        each(others, lambda n: copy_b(g, n).wait_send())
        for copy in (copy_far, copy_core, copy_on):
            copy(g).wait_send()
    for g in range(groups):
        each(others, lambda n: copy_d(g, n).wait_recv())
        filter_y(ky, recv_d, deep, g)

    def adjoint(u):
        return dot(kz[...], deep[:, u].reshape(depth, LANES)).astype(BF16)

    def send_last(n):
        stage_e[target(n)] = adjoint(target(n))
        copy_e(n).start()

    each(others, send_last)
    recv_e[others] = adjoint(h)

    def member(n):
        if blocks > 1:
            return n
        return source(n)

    if blocks > 1:
        each(others, lambda n: copy_e(n).wait_recv())
    turns = [own - 1] + list(range(own - 1))
    for n in turns:
        k = member(n)
        if blocks == 1:
            if n < others:
                copy_e(n).wait_recv()
            field = recv_e[n]
        else:
            field = jnp.concatenate(
                [recv_e[source(n * blocks + c)] for c in range(blocks)], axis=1
            )
        field = (field.astype(F32) * sea[...]).astype(BF16)
        m = s * own + k
        out[m] = (
            control[k].astype(F32) + weight[...] * dot(field, inv_x[...], 1, 1)
        ).astype(BF16)
        copy_last(0, n, m, far).start()
        copy_last(1, n, m, sib).start()
    for n in turns:
        copy_last(0, n, s * own + member(n), far).wait_recv()
        copy_last(2, n, far * own + member(n), sib).start()
    for g in range(groups):
        each(others, lambda n: copy_d(g, n).wait_send())
        copy_sum(g, 0).wait_send()
        copy_sum(g, 1).wait_send()
        copy_x(g).wait_send()
    each(others, lambda n: copy_e(n).wait_send())
    for n in turns:
        for phase, slot, peer in ((0, s, far), (1, s, sib), (2, far, sib)):
            copy = copy_last(phase, n, slot * own + member(n), peer)
            copy.wait_send()
            if phase > 0:
                copy.wait_recv()


def store_kernel(src, dst, held, sems):
    count = held.shape[0]
    size = src.shape[0] // count
    loads, stores = [], []
    for i in range(count):
        where = pl.ds(i * size, size)
        loads.append(pltpu.make_async_copy(src.at[where], held.at[i], sems.at[0, i]))
        stores.append(pltpu.make_async_copy(held.at[i], dst.at[where], sems.at[1, i]))
        loads[-1].start()
    for load, store in zip(loads, stores):
        load.wait()
        store.start()
    for store in stores:
        store.wait()


def per_device(
    slots,
    tiles,
    control,
    land_mask,
    tile_id,
    tile_scale,
    inverse_x,
    inverse_y,
    inverse_z,
    perturbations,
    obs_cell,
    obs_value,
    obs_weight,
):
    members, levels, rows, cols = control.shape
    depth = levels * rows
    blocks = cols // LANES
    assert slots == 4 and cols % LANES == 0 and cols & (cols - 1) == 0
    assert members // slots * blocks == tiles and depth % GROUP == 0 and 4 % rows == 0
    groups = next(n for n in (2, 1) if depth % (n * GROUP) == 0)
    piece = (depth // groups, LANES)
    units = (groups, tiles) + piece
    whole = pl.BlockSpec(memory_space=pl.ANY)
    vmem = pl.BlockSpec(memory_space=pltpu.VMEM)
    gradient = pl.pallas_call(
        functools.partial(kernel, slots, tiles, rows, groups),
        out_shape=jax.ShapeDtypeStruct((members, depth, cols), BF16),
        in_specs=[whole] + [vmem] * 6 + [whole] + [vmem] * 3,
        out_specs=vmem,
        scratch_shapes=[
            pltpu.VMEM((members // slots, depth, cols), BF16),
            pltpu.VMEM((members, depth, cols), BF16),
            pltpu.VMEM((depth, cols), F32),
            pltpu.VMEM((depth, cols), F32),
            pltpu.VMEM((tiles * GROUP, tiles * GROUP), BF16),
            pltpu.VMEM((tiles * GROUP, tiles * GROUP), BF16),
            pltpu.VMEM((depth, depth), BF16),
            pltpu.VMEM((depth, depth), BF16),
            pltpu.VMEM((4 * cols, depth), F32),
            pltpu.VMEM((2, depth, cols), F32),
            pltpu.VMEM((depth, cols), F32),
            pltpu.VMEM((depth, cols), F32),
            pltpu.VMEM(units, BF16),
            pltpu.VMEM(units, BF16),
            pltpu.VMEM(units, BF16),
            pltpu.VMEM((groups, slots, tiles) + piece, BF16),
            pltpu.VMEM((groups, 2, tiles) + piece, BF16),
            pltpu.VMEM((groups, 2, tiles) + piece, BF16),
            pltpu.VMEM(units, BF16),
            pltpu.VMEM(units, BF16),
            pltpu.VMEM(units, BF16),
            pltpu.VMEM(units, BF16),
            pltpu.VMEM(units, BF16),
            pltpu.VMEM((tiles, depth, LANES), BF16),
            pltpu.VMEM((tiles, depth, LANES), BF16),
            pltpu.SemaphoreType.DMA((4, groups, tiles)),
            pltpu.SemaphoreType.DMA((4, groups, tiles)),
            pltpu.SemaphoreType.DMA((6, groups)),
            pltpu.SemaphoreType.DMA((6, groups)),
            pltpu.SemaphoreType.DMA((3, members // slots)),
            pltpu.SemaphoreType.DMA((3, members // slots)),
            pltpu.SemaphoreType.DMA((2,)),
        ],
        compiler_params=pltpu.CompilerParams(
            collective_id=0, has_side_effects=True, vmem_limit_bytes=56 * 1024 * 1024
        ),
    )(
        control.reshape(members, depth, cols),
        land_mask.reshape(depth, cols),
        tile_id,
        tile_scale,
        inverse_x,
        inverse_y,
        inverse_z,
        perturbations.reshape(members, depth, cols),
        obs_cell,
        obs_value,
        obs_weight,
    )
    gradient = pl.pallas_call(
        store_kernel,
        out_shape=jax.ShapeDtypeStruct(gradient.shape, BF16),
        in_specs=[whole],
        out_specs=whole,
        scratch_shapes=[
            pltpu.VMEM((8, members // 8, depth, cols), BF16),
            pltpu.SemaphoreType.DMA((2, 8)),
        ],
        compiler_params=pltpu.CompilerParams(vmem_limit_bytes=56 * 1024 * 1024),
    )(gradient)
    return gradient.reshape(members, levels, rows, cols)


def solution(mesh):
    return jax.shard_map(
        functools.partial(per_device, mesh.shape["slot"], mesh.shape["horiz"]),
        mesh=mesh,
        in_specs=(
            P(None, None, "horiz", None),
            P(None, "horiz", None),
            P(),
            P(),
            P(),
            P(),
            P(),
            P("slot", None, None, "horiz", None),
            P("slot", "horiz"),
            P("slot", "horiz"),
            P("slot", "horiz"),
        ),
        out_specs=P(None, None, "horiz", None),
        check_vma=False,
    )
```

```python
import functools
import math

import jax
import jax.numpy as jnp
from jax import lax
from jax.experimental import pallas as pl
from jax.experimental.pallas import tpu as pltpu
from jax.sharding import PartitionSpec as P

LANES = 128
GROUP = 16
F32 = jnp.float32
BF16 = jnp.bfloat16
MESH = pl.DeviceIdType.MESH


def dot(a, b, ca=1, cb=0, precision=None):
    return lax.dot_general(
        a, b, (((ca,), (cb,)), ((), ())), preferred_element_type=F32, precision=precision
    )


def iota(shape, dim):
    return lax.broadcasted_iota(jnp.int32, shape, dim)


def spread_matrix(shape, index):
    return jnp.where(index == iota(shape, 1), 1.0, 0.0).astype(BF16)


def kernel(
    slots,
    tiles,
    rows,
    groups,
    control_hbm,
    land,
    tile_id,
    tile_scale,
    inv_x,
    inv_y,
    inv_z,
    pert_hbm,
    cells,
    values,
    weights,
    out,
    control,
    pert,
    sea,
    weight,
    ky,
    ky_t,
    kz,
    kz_t,
    obs_acc,
    cell_sum,
    inc,
    adj,
    send_a,
    recv_a,
    send_b,
    spread,
    stage_c,
    recv_c,
    stage_x,
    recv_x,
    stage_d,
    recv_d,
    deep,
    stage_e,
    recv_e,
    tile_ss,
    tile_rs,
    slot_ss,
    slot_rs,
    last_ss,
    last_rs,
    load_sem,
):
    members, depth, cols = control_hbm.shape
    own = members // slots
    blocks = cols // LANES
    levels = depth // rows
    part = depth // groups
    s = lax.axis_index("slot")
    h = lax.axis_index("horiz")
    sib = s + 1 - 2 * lax.rem(s, 2)
    far = s + 2 - 4 * (s // 2)
    diag = sib + 2 - 4 * (sib // 2)

    barrier = pltpu.get_barrier_semaphore()
    for d in range(1, tiles):
        pl.semaphore_signal(
            barrier, inc=1, device_id={"horiz": lax.rem(h + d, tiles)}, device_id_type=MESH
        )
    for peer in (sib, far):
        pl.semaphore_signal(barrier, inc=1, device_id={"slot": peer}, device_id_type=MESH)

    load_control = pltpu.make_async_copy(
        control_hbm.at[pl.ds(s * own, own)], control, load_sem.at[0]
    )
    load_pert = pltpu.make_async_copy(pert_hbm, pert, load_sem.at[1])
    load_control.start()
    load_pert.start()

    def distance(n):
        return tiles // 2 + (1 - 2 * (n % 2)) * ((n + 1) // 2)

    def target(n):
        return lax.rem(h + distance(n), tiles)

    def source(n):
        return lax.rem(h - distance(n) + tiles, tiles)

    def each(count, body):
        if count <= 8:
            for n in range(count):
                body(n)
        else:
            lax.fori_loop(0, count, lambda n, carry: (body(n), carry)[1], 0)

    def at_block(ref, c, where=slice(None)):
        if blocks == 1:
            return ref[where]
        return ref[where, pl.ds(pl.multiple_of(c * LANES, LANES), LANES)]

    def pert_rows(slot, unit, where):
        k, c = unit // blocks, lax.rem(unit, blocks)
        if blocks == 1:
            return pert[slot * own + k, where].astype(F32)
        lanes = pl.ds(pl.multiple_of(c * LANES, LANES), LANES)
        return pert[slot * own + k, where, lanes].astype(F32)

    def rows_of(g):
        return slice(g * part, (g + 1) * part)

    def to_tile(phase, g, n, src, dst):
        return pltpu.make_async_remote_copy(
            src_ref=src,
            dst_ref=dst,
            send_sem=tile_ss.at[phase, g, n],
            recv_sem=tile_rs.at[phase, g, n],
            device_id={"horiz": target(n)},
            device_id_type=MESH,
        )

    def to_slot(phase, g, n, src, dst, peer):
        return pltpu.make_async_remote_copy(
            src_ref=src,
            dst_ref=dst,
            send_sem=slot_ss.at[phase, g, n],
            recv_sem=slot_rs.at[phase, g, n],
            device_id={"slot": peer},
            device_id_type=MESH,
        )

    def copy_a(g, n):
        return to_tile(0, g, n, send_a.at[g, n], recv_a.at[g, h])

    def copy_b(g, n):
        return to_tile(1, g, n, send_b.at[g, target(n)], spread.at[g, s, n])

    def copy_d(n):
        return to_tile(2, 0, n, stage_d.at[n], recv_d.at[h])

    def copy_e(n):
        return to_tile(3, 0, n, stage_e.at[target(n)], recv_e.at[h])

    def copy_far(g, n):
        return to_slot(0, g, n, spread.at[g, s, n], spread.at[g, s, n], far)

    def copy_core(g, n):
        return to_slot(1, g, n, spread.at[g, s, n], spread.at[g, s, n], sib)

    def copy_on(g, n):
        return to_slot(2, g, n, spread.at[g, far, n], spread.at[g, far, n], sib)

    def copy_sum(i, n):
        return to_slot(3 + i, 0, n, stage_c.at[i, n], recv_c.at[i, n], sib)

    def copy_x(n):
        return to_slot(5, 0, n, stage_x.at[n], recv_x.at[n], far)

    def copy_last(phase, n, m, peer):
        return pltpu.make_async_remote_copy(
            src_ref=out.at[m],
            dst_ref=out.at[m],
            send_sem=last_ss.at[phase, n],
            recv_sem=last_rs.at[phase, n],
            device_id={"slot": peer},
            device_id_type=MESH,
        )

    others = tiles - 1

    region = tile_id[pl.ds(h * rows // 4, 1), :].astype(F32).astype(BF16)
    blocks_x = tile_id.shape[1]
    widen = jnp.where(iota((blocks_x, cols), 1) // 4 == iota((blocks_x, cols), 0), 1.0, 0.0)
    region_x = dot(region, widen.astype(BF16))
    regions = tile_scale.shape[0]
    onehot = jnp.where(iota((regions, cols), 0).astype(F32) == region_x, 1.0, 0.0)
    to_level = spread_matrix((depth, levels), iota((depth, levels), 0) // rows)
    scale_rows = dot(
        to_level.astype(F32), tile_scale[...], 1, 1, precision=lax.Precision.HIGHEST
    )
    sea[...] = land[...].astype(F32)
    weight[...] = sea[...] * dot(scale_rows, onehot, precision=lax.Precision.HIGHEST)

    same = lax.rem(iota((depth, depth), 0), rows) == lax.rem(iota((depth, depth), 1), rows)
    half = dot(to_level, inv_z[...], 1, 1).astype(BF16)
    kz_t[...] = jnp.where(same, dot(half, to_level, 1, 1), 0.0).astype(BF16)

    load_control.wait()

    def forward(n):
        u = target(n)
        k, c = u // blocks, lax.rem(u, blocks)
        masked = (weight[...] * control[k].astype(F32)).astype(BF16)
        along = (at_block(sea, c) * dot(masked, at_block(inv_x, c))).astype(BF16)
        return dot(kz_t[...], along).astype(BF16).reshape(groups, part, LANES)

    pl.semaphore_wait(barrier, tiles - 1 + 2)

    def send_first(n):
        send_a[:, n] = forward(n)
        copy_a(0, n).start()

    each(others, send_first)
    for g in range(1, groups):
        each(others, lambda n: copy_a(g, n).start())
    mine = forward(others)
    for g in range(groups):
        recv_a[g, h] = mine[g]

    wide = tiles * GROUP
    side = tiles * rows
    pos = iota((wide, side), 0)
    pick_y = spread_matrix((wide, side), pos // GROUP * rows + lax.rem(pos, rows))
    row_i, col_i = iota((wide, wide), 0), iota((wide, wide), 1)
    same_level = lax.rem(row_i, GROUP) // rows == lax.rem(col_i, GROUP) // rows
    half = dot(pick_y, inv_y[...], 1, 1).astype(BF16)
    ky_t[...] = jnp.where(same_level, dot(half, pick_y, 1, 1), 0.0).astype(BF16)

    def filter_y(matrix, src, dst, g):
        for i in range(part // GROUP):
            some = src[g, :, i * GROUP : (i + 1) * GROUP, :].reshape(wide, LANES)
            dst[g, :, i * GROUP : (i + 1) * GROUP, :] = (
                dot(matrix[...], some).astype(BF16).reshape(tiles, GROUP, LANES)
            )

    count = cells.shape[1]
    step = min(1024, count)
    chunks = count // step
    shift = cols.bit_length() - 1
    obs_acc[...] = jnp.zeros_like(obs_acc)

    def observe(i, carry):
        where = pl.ds(pl.multiple_of(i * step, step), step)
        cell, w = cells[:, where], weights[:, where]
        wv = w * values[:, where]
        w_hi = w.astype(BF16).astype(F32)
        v_hi = wv.astype(BF16).astype(F32)
        on_row = jnp.where(iota((depth, step), 0) == (cell >> shift), 1.0, 0.0).astype(BF16)
        on_col = iota((cols, step), 0) == (cell & (cols - 1))
        parts = [
            jnp.where(on_col, x, 0.0).astype(BF16) for x in (w_hi, w - w_hi, v_hi, wv - v_hi)
        ]
        obs_acc[...] += dot(jnp.concatenate(parts, axis=0), on_row, 1, 1)
        return carry

    ahead = chunks // 2
    lax.fori_loop(0, ahead, observe, 0)
    inc[...] = jnp.zeros_like(inc)

    for g in range(groups):
        each(others, lambda n: copy_a(g, n).wait_recv())
        filter_y(ky_t, recv_a, send_b, g)
        each(others, lambda n: copy_b(g, n).start())
        spread[g, s, others] = send_b[g, h]
    lax.fori_loop(ahead, chunks, observe, 0)
    for i in range(2):
        both = obs_acc[2 * i * cols : (2 * i + 1) * cols]
        both += obs_acc[(2 * i + 1) * cols : (2 * i + 2) * cols]
        cell_sum[i] = both.T
    load_pert.wait()

    norm = 1.0 / math.sqrt(members)

    def add_unit(g, slot, n):
        where = rows_of(g)
        unit = source(n)
        term = pert_rows(slot, unit, where) * spread[g, slot, n].astype(F32)
        if blocks == 1:
            inc[where] += term
        else:
            c = lax.rem(unit, blocks)
            inc[where, pl.ds(pl.multiple_of(c * LANES, LANES), LANES)] += term

    def gather(g, n):
        if not isinstance(n, int) or n < others:
            copy_b(g, n).wait_recv()
        copy_far(g, n).start()
        copy_core(g, n).start()
        add_unit(g, s, n)

    def pass_on(g, n):
        copy_far(g, n).wait_recv()
        copy_on(g, n).start()
        add_unit(g, far, n)
        copy_core(g, n).wait_recv()
        add_unit(g, sib, n)

    def finish(g, n):
        copy_on(g, n).wait_recv()
        add_unit(g, diag, n)

    for g in range(groups):
        copy_far(g, others).start()
        copy_core(g, others).start()
        add_unit(g, s, others)
        each(others, lambda n: gather(g, n))
    half = dot(pick_y, inv_y[...]).astype(BF16)
    ky[...] = jnp.where(same_level, dot(half, pick_y, 1, 1), 0.0).astype(BF16)
    half = dot(to_level, inv_z[...]).astype(BF16)
    kz[...] = jnp.where(same, dot(half, to_level, 1, 1), 0.0).astype(BF16)
    for g in range(groups):
        pass_on(g, others)
        each(others, lambda n: pass_on(g, n))
    for g in range(groups):
        finish(g, others)
        each(others, lambda n: finish(g, n))
    adj[...] = sea[...] * ((inc[...] * norm * cell_sum[0] - cell_sum[1]) * norm)

    def partial(slot, n):
        u = target(n)
        return pert_rows(slot, u, slice(None)) * at_block(adj, lax.rem(u, blocks))

    for i, slot in enumerate((diag, sib)):

        def to_core(n):
            stage_c[i, n] = partial(slot, n).astype(BF16)
            copy_sum(i, n).start()

        each(tiles, to_core)

    def between_chips(n):
        copy_sum(0, n).wait_recv()
        stage_x[n] = (partial(far, n) + recv_c[0, n].astype(F32)).astype(BF16)
        copy_x(n).start()

    each(tiles, between_chips)

    def total(n):
        copy_sum(1, n).wait_recv()
        copy_x(n).wait_recv()
        value = partial(s, n) + recv_c[1, n].astype(F32) + recv_x[n].astype(F32)
        return value.astype(BF16)

    def exchange(n):
        stage_d[n] = total(n)
        copy_d(n).start()

    each(others, exchange)
    recv_d[h] = total(others)

    for g in range(groups):
        each(others, lambda n: copy_a(g, n).wait_send())
        each(others, lambda n: copy_b(g, n).wait_send())
        for copy in (copy_far, copy_core, copy_on):
            each(tiles, lambda n: copy(g, n).wait_send())

    def adjoint_z(u):
        deep[u] = dot(kz[...], recv_d[u]).astype(BF16)

    def arrived(n):
        copy_d(n).wait_recv()
        adjoint_z(source(n))

    adjoint_z(h)
    each(others, arrived)
    for i in range(depth // GROUP):
        where = slice(i * GROUP, (i + 1) * GROUP)
        some = deep[:, where, :].reshape(wide, LANES)
        stage_e[:, where, :] = dot(ky[...], some).astype(BF16).reshape(tiles, GROUP, LANES)
    each(others, lambda n: copy_e(n).start())
    recv_e[h] = stage_e[h]

    def member(n):
        if blocks > 1:
            return n
        return source(n)

    if blocks > 1:
        each(others, lambda n: copy_e(n).wait_recv())
    turns = [own - 1] + list(range(own - 1))
    for n in turns:
        k = member(n)
        if blocks == 1:
            if n < others:
                copy_e(n).wait_recv()
            field = recv_e[k]
        else:
            field = jnp.concatenate(
                [recv_e[n * blocks + c] for c in range(blocks)], axis=1
            )
        field = (field.astype(F32) * sea[...]).astype(BF16)
        m = s * own + k
        out[m] = (
            control[k].astype(F32) + weight[...] * dot(field, inv_x[...], 1, 1)
        ).astype(BF16)
        copy_last(0, n, m, far).start()
        copy_last(1, n, m, sib).start()
    for n in turns:
        copy_last(0, n, s * own + member(n), far).wait_recv()
        copy_last(2, n, far * own + member(n), sib).start()
    each(others, lambda n: copy_d(n).wait_send())
    each(others, lambda n: copy_e(n).wait_send())
    for copy in (lambda n: copy_sum(0, n), lambda n: copy_sum(1, n), copy_x):
        each(tiles, lambda n: copy(n).wait_send())
    for n in turns:
        for phase, slot, peer in ((0, s, far), (1, s, sib), (2, far, sib)):
            copy = copy_last(phase, n, slot * own + member(n), peer)
            copy.wait_send()
            if phase > 0:
                copy.wait_recv()


def store_kernel(src, dst, held, sems):
    count = held.shape[0]
    size = src.shape[0] // count
    loads, stores = [], []
    for i in range(count):
        where = pl.ds(i * size, size)
        loads.append(pltpu.make_async_copy(src.at[where], held.at[i], sems.at[0, i]))
        stores.append(pltpu.make_async_copy(held.at[i], dst.at[where], sems.at[1, i]))
        loads[-1].start()
    for load, store in zip(loads, stores):
        load.wait()
        store.start()
    for store in stores:
        store.wait()


def per_device(
    slots,
    tiles,
    control,
    land_mask,
    tile_id,
    tile_scale,
    inverse_x,
    inverse_y,
    inverse_z,
    perturbations,
    obs_cell,
    obs_value,
    obs_weight,
):
    members, levels, rows, cols = control.shape
    depth = levels * rows
    blocks = cols // LANES
    assert slots == 4 and cols % LANES == 0 and cols & (cols - 1) == 0
    assert members // slots * blocks == tiles and depth % GROUP == 0 and 4 % rows == 0
    groups = next(n for n in (2, 1) if depth % (n * GROUP) == 0)
    piece = (depth // groups, LANES)
    units = (groups, tiles) + piece
    columns = (tiles, depth, LANES)
    whole = pl.BlockSpec(memory_space=pl.ANY)
    vmem = pl.BlockSpec(memory_space=pltpu.VMEM)
    gradient = pl.pallas_call(
        functools.partial(kernel, slots, tiles, rows, groups),
        out_shape=jax.ShapeDtypeStruct((members, depth, cols), BF16),
        in_specs=[whole] + [vmem] * 6 + [whole] + [vmem] * 3,
        out_specs=vmem,
        scratch_shapes=[
            pltpu.VMEM((members // slots, depth, cols), BF16),
            pltpu.VMEM((members, depth, cols), BF16),
            pltpu.VMEM((depth, cols), F32),
            pltpu.VMEM((depth, cols), F32),
            pltpu.VMEM((tiles * GROUP, tiles * GROUP), BF16),
            pltpu.VMEM((tiles * GROUP, tiles * GROUP), BF16),
            pltpu.VMEM((depth, depth), BF16),
            pltpu.VMEM((depth, depth), BF16),
            pltpu.VMEM((4 * cols, depth), F32),
            pltpu.VMEM((2, depth, cols), F32),
            pltpu.VMEM((depth, cols), F32),
            pltpu.VMEM((depth, cols), F32),
            pltpu.VMEM(units, BF16),
            pltpu.VMEM(units, BF16),
            pltpu.VMEM(units, BF16),
            pltpu.VMEM((groups, slots, tiles) + piece, BF16),
            pltpu.VMEM((2,) + columns, BF16),
            pltpu.VMEM((2,) + columns, BF16),
            pltpu.VMEM(columns, BF16),
            pltpu.VMEM(columns, BF16),
            pltpu.VMEM(columns, BF16),
            pltpu.VMEM(columns, BF16),
            pltpu.VMEM(columns, BF16),
            pltpu.VMEM(columns, BF16),
            pltpu.VMEM(columns, BF16),
            pltpu.SemaphoreType.DMA((4, groups, tiles)),
            pltpu.SemaphoreType.DMA((4, groups, tiles)),
            pltpu.SemaphoreType.DMA((6, groups, tiles)),
            pltpu.SemaphoreType.DMA((6, groups, tiles)),
            pltpu.SemaphoreType.DMA((3, members // slots)),
            pltpu.SemaphoreType.DMA((3, members // slots)),
            pltpu.SemaphoreType.DMA((2,)),
        ],
        compiler_params=pltpu.CompilerParams(
            collective_id=0, has_side_effects=True, vmem_limit_bytes=56 * 1024 * 1024
        ),
    )(
        control.reshape(members, depth, cols),
        land_mask.reshape(depth, cols),
        tile_id,
        tile_scale,
        inverse_x,
        inverse_y,
        inverse_z,
        perturbations.reshape(members, depth, cols),
        obs_cell,
        obs_value,
        obs_weight,
    )
    gradient = pl.pallas_call(
        store_kernel,
        out_shape=jax.ShapeDtypeStruct(gradient.shape, BF16),
        in_specs=[whole],
        out_specs=whole,
        scratch_shapes=[
            pltpu.VMEM((8, members // 8, depth, cols), BF16),
            pltpu.SemaphoreType.DMA((2, 8)),
        ],
        compiler_params=pltpu.CompilerParams(vmem_limit_bytes=56 * 1024 * 1024),
    )(gradient)
    return gradient.reshape(members, levels, rows, cols)


def solution(mesh):
    return jax.shard_map(
        functools.partial(per_device, mesh.shape["slot"], mesh.shape["horiz"]),
        mesh=mesh,
        in_specs=(
            P(None, None, "horiz", None),
            P(None, "horiz", None),
            P(),
            P(),
            P(),
            P(),
            P(),
            P("slot", None, None, "horiz", None),
            P("slot", "horiz"),
            P("slot", "horiz"),
            P("slot", "horiz"),
        ),
        out_specs=P(None, None, "horiz", None),
        check_vma=False,
    )
```

```python
import functools
import math

import jax
import jax.numpy as jnp
from jax import lax
from jax.experimental import pallas as pl
from jax.experimental.pallas import tpu as pltpu
from jax.sharding import PartitionSpec as P

LANES = 128
GROUP = 16
F32 = jnp.float32
BF16 = jnp.bfloat16
MESH = pl.DeviceIdType.MESH


def dot(a, b, ca=1, cb=0, precision=None):
    return lax.dot_general(
        a, b, (((ca,), (cb,)), ((), ())), preferred_element_type=F32, precision=precision
    )


def iota(shape, dim):
    return lax.broadcasted_iota(jnp.int32, shape, dim)


def spread_matrix(shape, index):
    return jnp.where(index == iota(shape, 1), 1.0, 0.0).astype(BF16)


def kernel(
    slots,
    tiles,
    rows,
    groups,
    control_hbm,
    land,
    tile_id,
    tile_scale,
    inv_x,
    inv_y,
    inv_z,
    pert_hbm,
    cells,
    values,
    weights,
    out,
    control,
    pert,
    sea,
    weight,
    ky,
    ky_t,
    kz,
    kz_t,
    obs_acc,
    cell_sum,
    inc,
    adj,
    send_a,
    recv_a,
    send_b,
    spread,
    stage_c,
    recv_c,
    stage_x,
    recv_x,
    stage_d,
    recv_d,
    deep,
    stage_e,
    recv_e,
    tile_ss,
    tile_rs,
    slot_ss,
    slot_rs,
    last_ss,
    last_rs,
    load_sem,
):
    members, depth, cols = control_hbm.shape
    own = members // slots
    blocks = cols // LANES
    levels = depth // rows
    part = depth // groups
    s = lax.axis_index("slot")
    h = lax.axis_index("horiz")
    sib = s + 1 - 2 * lax.rem(s, 2)
    far = s + 2 - 4 * (s // 2)
    diag = sib + 2 - 4 * (sib // 2)

    barrier = pltpu.get_barrier_semaphore()
    for d in range(1, tiles):
        pl.semaphore_signal(
            barrier, inc=1, device_id={"horiz": lax.rem(h + d, tiles)}, device_id_type=MESH
        )
    for peer in (sib, far):
        pl.semaphore_signal(barrier, inc=1, device_id={"slot": peer}, device_id_type=MESH)

    load_control = pltpu.make_async_copy(
        control_hbm.at[pl.ds(s * own, own)], control, load_sem.at[0]
    )
    load_pert = pltpu.make_async_copy(pert_hbm, pert, load_sem.at[1])
    load_control.start()
    load_pert.start()

    def distance(n):
        return tiles // 2 + (1 - 2 * (n % 2)) * ((n + 1) // 2)

    def target(n):
        return lax.rem(h + distance(n), tiles)

    def source(n):
        return lax.rem(h - distance(n) + tiles, tiles)

    def each(count, body):
        if count <= 8:
            for n in range(count):
                body(n)
        else:
            lax.fori_loop(0, count, lambda n, carry: (body(n), carry)[1], 0)

    def at_block(ref, c, where=slice(None)):
        if blocks == 1:
            return ref[where]
        return ref[where, pl.ds(pl.multiple_of(c * LANES, LANES), LANES)]

    def pert_rows(slot, unit, where):
        k, c = unit // blocks, lax.rem(unit, blocks)
        if blocks == 1:
            return pert[slot * own + k, where].astype(F32)
        lanes = pl.ds(pl.multiple_of(c * LANES, LANES), LANES)
        return pert[slot * own + k, where, lanes].astype(F32)

    def rows_of(g):
        return slice(g * part, (g + 1) * part)

    def to_tile(phase, g, n, src, dst):
        return pltpu.make_async_remote_copy(
            src_ref=src,
            dst_ref=dst,
            send_sem=tile_ss.at[phase, g, n],
            recv_sem=tile_rs.at[phase, g, n],
            device_id={"horiz": target(n)},
            device_id_type=MESH,
        )

    def to_slot(phase, g, n, src, dst, peer):
        return pltpu.make_async_remote_copy(
            src_ref=src,
            dst_ref=dst,
            send_sem=slot_ss.at[phase, g, n],
            recv_sem=slot_rs.at[phase, g, n],
            device_id={"slot": peer},
            device_id_type=MESH,
        )

    def copy_a(g, n):
        return to_tile(0, g, n, send_a.at[g, n], recv_a.at[g, h])

    def copy_b(g, n):
        return to_tile(1, g, n, send_b.at[g, target(n)], spread.at[g, s, n])

    def copy_d(n):
        return to_tile(2, 0, n, stage_d.at[n], recv_d.at[h])

    def copy_e(n):
        return to_tile(3, 0, n, stage_e.at[target(n)], recv_e.at[h])

    def two(n):
        return pl.ds(2 * n, 2)

    def copy_far(g, n):
        return to_slot(0, g, n, spread.at[g, s, two(n)], spread.at[g, s, two(n)], far)

    def copy_core(g, n):
        return to_slot(1, g, n, spread.at[g, s, two(n)], spread.at[g, s, two(n)], sib)

    def copy_on(g, n):
        return to_slot(2, g, n, spread.at[g, far, two(n)], spread.at[g, far, two(n)], sib)

    def copy_sum(i, n):
        return to_slot(3 + i, 0, n, stage_c.at[i, two(n)], recv_c.at[i, two(n)], sib)

    def copy_x(n):
        return to_slot(5, 0, n, stage_x.at[two(n)], recv_x.at[two(n)], far)

    def copy_last(phase, n, m, peer):
        return pltpu.make_async_remote_copy(
            src_ref=out.at[m],
            dst_ref=out.at[m],
            send_sem=last_ss.at[phase, n],
            recv_sem=last_rs.at[phase, n],
            device_id={"slot": peer},
            device_id_type=MESH,
        )

    others = tiles - 1

    region = tile_id[pl.ds(h * rows // 4, 1), :].astype(F32).astype(BF16)
    blocks_x = tile_id.shape[1]
    widen = jnp.where(iota((blocks_x, cols), 1) // 4 == iota((blocks_x, cols), 0), 1.0, 0.0)
    region_x = dot(region, widen.astype(BF16))
    regions = tile_scale.shape[0]
    onehot = jnp.where(iota((regions, cols), 0).astype(F32) == region_x, 1.0, 0.0)
    to_level = spread_matrix((depth, levels), iota((depth, levels), 0) // rows)
    scale_rows = dot(
        to_level.astype(F32), tile_scale[...], 1, 1, precision=lax.Precision.HIGHEST
    )
    sea[...] = land[...].astype(F32)
    weight[...] = sea[...] * dot(scale_rows, onehot, precision=lax.Precision.HIGHEST)

    same = lax.rem(iota((depth, depth), 0), rows) == lax.rem(iota((depth, depth), 1), rows)
    half = dot(to_level, inv_z[...], 1, 1).astype(BF16)
    kz_t[...] = jnp.where(same, dot(half, to_level, 1, 1), 0.0).astype(BF16)

    load_control.wait()

    def forward(n):
        u = target(n)
        k, c = u // blocks, lax.rem(u, blocks)
        masked = (weight[...] * control[k].astype(F32)).astype(BF16)
        along = (at_block(sea, c) * dot(masked, at_block(inv_x, c))).astype(BF16)
        return dot(kz_t[...], along).astype(BF16).reshape(groups, part, LANES)

    pl.semaphore_wait(barrier, tiles - 1 + 2)

    def send_first(n):
        send_a[:, n] = forward(n)
        copy_a(0, n).start()

    each(others, send_first)
    for g in range(1, groups):
        each(others, lambda n: copy_a(g, n).start())
    mine = forward(others)
    for g in range(groups):
        recv_a[g, h] = mine[g]

    wide = tiles * GROUP
    side = tiles * rows
    pos = iota((wide, side), 0)
    pick_y = spread_matrix((wide, side), pos // GROUP * rows + lax.rem(pos, rows))
    row_i, col_i = iota((wide, wide), 0), iota((wide, wide), 1)
    same_level = lax.rem(row_i, GROUP) // rows == lax.rem(col_i, GROUP) // rows
    half = dot(pick_y, inv_y[...], 1, 1).astype(BF16)
    ky_t[...] = jnp.where(same_level, dot(half, pick_y, 1, 1), 0.0).astype(BF16)

    def filter_y(matrix, src, dst, g):
        for i in range(part // GROUP):
            some = src[g, :, i * GROUP : (i + 1) * GROUP, :].reshape(wide, LANES)
            dst[g, :, i * GROUP : (i + 1) * GROUP, :] = (
                dot(matrix[...], some).astype(BF16).reshape(tiles, GROUP, LANES)
            )

    count = cells.shape[1]
    step = min(1024, count)
    chunks = count // step
    shift = cols.bit_length() - 1
    obs_acc[...] = jnp.zeros_like(obs_acc)

    def observe(i, carry):
        where = pl.ds(pl.multiple_of(i * step, step), step)
        cell, w = cells[:, where], weights[:, where]
        wv = w * values[:, where]
        w_hi = w.astype(BF16).astype(F32)
        v_hi = wv.astype(BF16).astype(F32)
        on_row = jnp.where(iota((depth, step), 0) == (cell >> shift), 1.0, 0.0).astype(BF16)
        on_col = iota((cols, step), 0) == (cell & (cols - 1))
        parts = [
            jnp.where(on_col, x, 0.0).astype(BF16) for x in (w_hi, w - w_hi, v_hi, wv - v_hi)
        ]
        obs_acc[...] += dot(jnp.concatenate(parts, axis=0), on_row, 1, 1)
        return carry

    ahead = chunks // 2
    lax.fori_loop(0, ahead, observe, 0)
    inc[...] = jnp.zeros_like(inc)

    for g in range(groups):
        each(others, lambda n: copy_a(g, n).wait_recv())
        filter_y(ky_t, recv_a, send_b, g)
        each(others, lambda n: copy_b(g, n).start())
        spread[g, s, others] = send_b[g, h]
    lax.fori_loop(ahead, chunks, observe, 0)
    for i in range(2):
        both = obs_acc[2 * i * cols : (2 * i + 1) * cols]
        both += obs_acc[(2 * i + 1) * cols : (2 * i + 2) * cols]
        cell_sum[i] = both.T
    load_pert.wait()

    norm = 1.0 / math.sqrt(members)

    def add_unit(g, slot, n):
        where = rows_of(g)
        unit = source(n)
        term = pert_rows(slot, unit, where) * spread[g, slot, n].astype(F32)
        if blocks == 1:
            inc[where] += term
        else:
            c = lax.rem(unit, blocks)
            inc[where, pl.ds(pl.multiple_of(c * LANES, LANES), LANES)] += term

    def gather(g, n, count):
        for i in range(count):
            copy_b(g, 2 * n + i).wait_recv()
        copy_far(g, n).start()
        copy_core(g, n).start()
        add_unit(g, s, 2 * n)
        add_unit(g, s, 2 * n + 1)

    def pass_on(g, n):
        copy_far(g, n).wait_recv()
        copy_on(g, n).start()
        add_unit(g, far, 2 * n)
        add_unit(g, far, 2 * n + 1)
        copy_core(g, n).wait_recv()
        add_unit(g, sib, 2 * n)
        add_unit(g, sib, 2 * n + 1)

    def finish(g, n):
        copy_on(g, n).wait_recv()
        add_unit(g, diag, 2 * n)
        add_unit(g, diag, 2 * n + 1)

    pairs = tiles // 2
    for g in range(groups):
        each(pairs - 1, lambda n: gather(g, n, 2))
        gather(g, pairs - 1, 1)
    half = dot(pick_y, inv_y[...]).astype(BF16)
    ky[...] = jnp.where(same_level, dot(half, pick_y, 1, 1), 0.0).astype(BF16)
    half = dot(to_level, inv_z[...]).astype(BF16)
    kz[...] = jnp.where(same, dot(half, to_level, 1, 1), 0.0).astype(BF16)
    for g in range(groups):
        each(pairs, lambda n: pass_on(g, n))
    for g in range(groups):
        each(pairs, lambda n: finish(g, n))
    adj[...] = sea[...] * ((inc[...] * norm * cell_sum[0] - cell_sum[1]) * norm)

    def partial(slot, n):
        u = target(n)
        return pert_rows(slot, u, slice(None)) * at_block(adj, lax.rem(u, blocks))

    for i, slot in enumerate((diag, sib)):

        def to_core(n):
            for m in (2 * n, 2 * n + 1):
                stage_c[i, m] = partial(slot, m).astype(BF16)
            copy_sum(i, n).start()

        each(pairs, to_core)

    def between_chips(n):
        copy_sum(0, n).wait_recv()
        for m in (2 * n, 2 * n + 1):
            stage_x[m] = (partial(far, m) + recv_c[0, m].astype(F32)).astype(BF16)
        copy_x(n).start()

    each(pairs, between_chips)

    def total(n):
        value = partial(s, n) + recv_c[1, n].astype(F32) + recv_x[n].astype(F32)
        return value.astype(BF16)

    def exchange(n, count):
        copy_sum(1, n).wait_recv()
        copy_x(n).wait_recv()
        for m in [2 * n, 2 * n + 1][:count]:
            stage_d[m] = total(m)
            copy_d(m).start()

    each(pairs - 1, lambda n: exchange(n, 2))
    exchange(pairs - 1, 1)
    recv_d[h] = total(others)

    for g in range(groups):
        each(others, lambda n: copy_a(g, n).wait_send())
        each(others, lambda n: copy_b(g, n).wait_send())
        for copy in (copy_far, copy_core, copy_on):
            each(pairs, lambda n: copy(g, n).wait_send())

    def adjoint_z(u):
        deep[u] = dot(kz[...], recv_d[u]).astype(BF16)

    def arrived(n):
        copy_d(n).wait_recv()
        adjoint_z(source(n))

    adjoint_z(h)
    each(others, arrived)
    for i in range(depth // GROUP):
        where = slice(i * GROUP, (i + 1) * GROUP)
        some = deep[:, where, :].reshape(wide, LANES)
        stage_e[:, where, :] = dot(ky[...], some).astype(BF16).reshape(tiles, GROUP, LANES)
    each(others, lambda n: copy_e(n).start())
    recv_e[h] = stage_e[h]
    each(others, lambda n: copy_d(n).wait_send())
    for copy in (lambda n: copy_sum(0, n), lambda n: copy_sum(1, n), copy_x):
        each(pairs, lambda n: copy(n).wait_send())

    def member(n):
        if blocks > 1:
            return n
        return source(n)

    if blocks > 1:
        each(others, lambda n: copy_e(n).wait_recv())
    turns = [own - 1] + list(range(own - 1))
    for n in turns:
        k = member(n)
        if blocks == 1:
            if n < others:
                copy_e(n).wait_recv()
            field = recv_e[k]
        else:
            field = jnp.concatenate(
                [recv_e[n * blocks + c] for c in range(blocks)], axis=1
            )
        field = (field.astype(F32) * sea[...]).astype(BF16)
        m = s * own + k
        out[m] = (
            control[k].astype(F32) + weight[...] * dot(field, inv_x[...], 1, 1)
        ).astype(BF16)
        copy_last(0, n, m, far).start()
        copy_last(1, n, m, sib).start()
    for n in turns:
        copy_last(0, n, s * own + member(n), far).wait_recv()
        copy_last(2, n, far * own + member(n), sib).start()
    each(others, lambda n: copy_e(n).wait_send())
    for n in turns:
        for phase, slot, peer in ((0, s, far), (1, s, sib), (2, far, sib)):
            copy = copy_last(phase, n, slot * own + member(n), peer)
            copy.wait_send()
            if phase > 0:
                copy.wait_recv()


def store_kernel(src, dst, held, sems):
    count = held.shape[0]
    size = src.shape[0] // count
    loads, stores = [], []
    for i in range(count):
        where = pl.ds(i * size, size)
        loads.append(pltpu.make_async_copy(src.at[where], held.at[i], sems.at[0, i]))
        stores.append(pltpu.make_async_copy(held.at[i], dst.at[where], sems.at[1, i]))
        loads[-1].start()
    for load, store in zip(loads, stores):
        load.wait()
        store.start()
    for store in stores:
        store.wait()


def per_device(
    slots,
    tiles,
    control,
    land_mask,
    tile_id,
    tile_scale,
    inverse_x,
    inverse_y,
    inverse_z,
    perturbations,
    obs_cell,
    obs_value,
    obs_weight,
):
    members, levels, rows, cols = control.shape
    depth = levels * rows
    blocks = cols // LANES
    assert slots == 4 and tiles % 2 == 0 and cols % LANES == 0 and cols & (cols - 1) == 0
    assert members // slots * blocks == tiles and depth % GROUP == 0 and 4 % rows == 0
    groups = next(n for n in (2, 1) if depth % (n * GROUP) == 0)
    piece = (depth // groups, LANES)
    units = (groups, tiles) + piece
    columns = (tiles, depth, LANES)
    whole = pl.BlockSpec(memory_space=pl.ANY)
    vmem = pl.BlockSpec(memory_space=pltpu.VMEM)
    gradient = pl.pallas_call(
        functools.partial(kernel, slots, tiles, rows, groups),
        out_shape=jax.ShapeDtypeStruct((members, depth, cols), BF16),
        in_specs=[whole] + [vmem] * 6 + [whole] + [vmem] * 3,
        out_specs=vmem,
        scratch_shapes=[
            pltpu.VMEM((members // slots, depth, cols), BF16),
            pltpu.VMEM((members, depth, cols), BF16),
            pltpu.VMEM((depth, cols), F32),
            pltpu.VMEM((depth, cols), F32),
            pltpu.VMEM((tiles * GROUP, tiles * GROUP), BF16),
            pltpu.VMEM((tiles * GROUP, tiles * GROUP), BF16),
            pltpu.VMEM((depth, depth), BF16),
            pltpu.VMEM((depth, depth), BF16),
            pltpu.VMEM((4 * cols, depth), F32),
            pltpu.VMEM((2, depth, cols), F32),
            pltpu.VMEM((depth, cols), F32),
            pltpu.VMEM((depth, cols), F32),
            pltpu.VMEM(units, BF16),
            pltpu.VMEM(units, BF16),
            pltpu.VMEM(units, BF16),
            pltpu.VMEM((groups, slots, tiles) + piece, BF16),
            pltpu.VMEM((2,) + columns, BF16),
            pltpu.VMEM((2,) + columns, BF16),
            pltpu.VMEM(columns, BF16),
            pltpu.VMEM(columns, BF16),
            pltpu.VMEM(columns, BF16),
            pltpu.VMEM(columns, BF16),
            pltpu.VMEM(columns, BF16),
            pltpu.VMEM(columns, BF16),
            pltpu.VMEM(columns, BF16),
            pltpu.SemaphoreType.DMA((4, groups, tiles)),
            pltpu.SemaphoreType.DMA((4, groups, tiles)),
            pltpu.SemaphoreType.DMA((6, groups, tiles)),
            pltpu.SemaphoreType.DMA((6, groups, tiles)),
            pltpu.SemaphoreType.DMA((3, members // slots)),
            pltpu.SemaphoreType.DMA((3, members // slots)),
            pltpu.SemaphoreType.DMA((2,)),
        ],
        compiler_params=pltpu.CompilerParams(
            collective_id=0, has_side_effects=True, vmem_limit_bytes=56 * 1024 * 1024
        ),
    )(
        control.reshape(members, depth, cols),
        land_mask.reshape(depth, cols),
        tile_id,
        tile_scale,
        inverse_x,
        inverse_y,
        inverse_z,
        perturbations.reshape(members, depth, cols),
        obs_cell,
        obs_value,
        obs_weight,
    )
    gradient = pl.pallas_call(
        store_kernel,
        out_shape=jax.ShapeDtypeStruct(gradient.shape, BF16),
        in_specs=[whole],
        out_specs=whole,
        scratch_shapes=[
            pltpu.VMEM((8, members // 8, depth, cols), BF16),
            pltpu.SemaphoreType.DMA((2, 8)),
        ],
        compiler_params=pltpu.CompilerParams(vmem_limit_bytes=56 * 1024 * 1024),
    )(gradient)
    return gradient.reshape(members, levels, rows, cols)


def solution(mesh):
    return jax.shard_map(
        functools.partial(per_device, mesh.shape["slot"], mesh.shape["horiz"]),
        mesh=mesh,
        in_specs=(
            P(None, None, "horiz", None),
            P(None, "horiz", None),
            P(),
            P(),
            P(),
            P(),
            P(),
            P("slot", None, None, "horiz", None),
            P("slot", "horiz"),
            P("slot", "horiz"),
            P("slot", "horiz"),
        ),
        out_specs=P(None, None, "horiz", None),
        check_vma=False,
    )
```
